512 devices in a mesh: group: 16 (over x_lo, y, core), tensor: 32 (over z, x_hi).
Axes of the slice: x: 4 (x_hi: 2, x_lo: 2; x = x_hi * 2 + x_lo), y: 4, z: 16, core: 2. Of those that a mesh axis runs over, the one named last changes fastest.
Arguments:
- hidden_in: bfloat16 [4, 4096, 5120], P(None, 'group', 'tensor'), may hold values from -6 to 6
- norm_gain: float32 [5120], replicated, may hold values from 0.25 to 1.75
- q_weight: bfloat16 [5120, 4096], P(None, 'tensor'), may hold values from -0.078125 to 0.078125
- q_gain: float32 [128], replicated, may hold values from 0.25 to 1.75
- o_weight: bfloat16 [4096, 5120], P(None, 'tensor'), may hold values from -0.09375 to 0.09375
- kv_cache: bfloat16 [2, 4096, 8, 512], P(None, 'group'), may hold values from -600 to 600
- positions: int32 [4, 4096], P(None, 'group'), may hold values from 0 to 4095
- grad_down: bfloat16 [16, 64, 5120], P('group', None, 'tensor'), may hold values from -6 to 6
- grad_up: bfloat16 [16, 64, 4096], P('group', None, 'tensor'), may hold values from -6 to 6
- down_param: float32 [64, 5120], P(None, 'tensor'), may hold values from -5 to 5
- down_first: float32 [64, 5120], P(None, 'tensor'), may hold values from -4 to 4
- down_second: float32 [64, 5120], P(None, 'tensor'), may hold values from 0.01 to 0.5
- up_param: float32 [64, 4096], P(None, 'tensor'), may hold values from -5 to 5
- up_first: float32 [64, 4096], P(None, 'tensor'), may hold values from -4 to 4
- up_second: float32 [64, 4096], P(None, 'tensor'), may hold values from 0.01 to 0.5
Outputs:
- new_down: float32 [64, 5120], P(None, 'tensor')
- new_up: float32 [64, 4096], P(None, 'tensor')
- decoded: bfloat16 [4, 4096, 5120], P(None, 'group', 'tensor')
The draws below stay inside these ranges and needn't reach their ends.
All inputs are finite; a program needn't handle non-finite values.
Results may differ from the reference program's by a relative error of at most 0.012.
The reference program's roundings to bfloat16 on the way (of `merged`, `normed`, `rotated`, `weights` and `heads_out`) count: a program that leaves them out, or rounds other values in their place, can miss the bound.
Values may be sent and summed in bfloat16 or wider, within the bound.
A program may use at most 64 MiB of HBM per device.

```python
import math
import jax
import jax.numpy as jnp
from jax import lax

D = 5120
HEAD = 128
R = 64
STEPS = 4
CACHE = 8
HEADS = 32
KVH = 4
KVF = 512
HQ = 4096
ROWS_ALL = 4096
PARTIALS = 16


def draw_kv_cache(key, part):
    key = jax.random.fold_in(key, 11)
    key_base = jax.random.fold_in(key, 0)
    base = jnp.clip(jax.random.normal(key_base, (2, ROWS_ALL, CACHE, KVF), jnp.float32), -4.0, 4.0)
    return base.astype(jnp.bfloat16)


def place_ends(values, stream_key, low, top_value):
    extent = values.shape
    index_at = [jax.random.randint(jax.random.fold_in(stream_key, axis), (), 0, extent[axis]) for axis in range(len(extent))]
    values = values.at[tuple(index_at)].set(low)
    longest = extent.index(max(extent))
    index_at[longest] = (index_at[longest] + 1) % extent[longest]
    return values.at[tuple(index_at)].set(top_value)


def with_spikes(entries, stream_key, source, target, parts, factor):
    owner, partner = [(jnp.arange(entries.shape[axis_at]) // (entries.shape[axis_at] // parts)).reshape([-1 if axis == axis_at else 1 for axis in range(entries.ndim)]) for axis_at in (source, target)]
    chosen = jax.random.permutation(stream_key, parts)[partner]
    strong = (owner == chosen) | (owner == (partner + parts // 2) % parts)
    return jnp.where(strong, factor * entries, entries)


def steps_of(rng, shape, cuts, least, top_value):
    def one(axis_at, parts):
        draws = jax.random.uniform(jax.random.fold_in(jax.random.fold_in(rng, 6), axis_at), (parts,), jnp.float32, least / len(cuts), top_value / len(cuts))
        return jnp.repeat(jnp.exp(draws), shape[axis_at] // parts).reshape((-1,) + (1,) * (len(shape) - axis_at - 1))

    factor_of = one(*cuts[0])
    for cut in cuts[1:]:
        factor_of = factor_of * one(*cut)
    return factor_of


def noise(stream_key, shape, spread, reach, pieces=(), kind=jnp.bfloat16):
    gain = steps_of(stream_key, shape, pieces, -0.22, 0.18) if pieces else 1.0
    array = jax.random.normal(stream_key, shape, jnp.float32) * spread * gain
    return jnp.minimum(jnp.maximum(array, -reach), reach).astype(kind)


def bell_draw_with(stream_key, dims, spread, reach, cuts, heavy, kind=jnp.bfloat16):
    entries = spread * jax.random.normal(stream_key, dims, jnp.float32)
    if cuts:
        entries = entries * steps_of(stream_key, dims, cuts, -0.22, 0.18)
    return jnp.clip(with_spikes(entries, jax.random.fold_in(stream_key, 3), *heavy), -reach, reach).astype(kind)


def setup_inputs(seed: int = 0) -> dict:
    key_of = jax.random.split(jax.random.key(seed), 16)
    return {
        "hidden_in": noise(key_of[0], (STEPS, ROWS_ALL, D), 1.0, 6.0, ((1, 16), (2, 32))),
        "norm_gain": jnp.clip(1.0 + 0.15 * jax.random.normal(key_of[1], (D,), jnp.float32), 0.25, 1.75),
        "q_weight": noise(key_of[2], (D, HQ), D ** -0.5, 0.078125, ((1, 32),)),
        "q_gain": jnp.clip(1.0 + 0.15 * jax.random.normal(key_of[3], (HEAD,), jnp.float32), 0.25, 1.75),
        "o_weight": noise(key_of[4], (HQ, D), HQ ** -0.5, 0.09375, ((1, 32),)),
        "kv_cache": draw_kv_cache(jax.random.fold_in(key_of[15], 71), 0),
        "positions": place_ends(jax.random.randint(key_of[6], (STEPS, ROWS_ALL), 0, 4096), jax.random.fold_in(key_of[6], 1), 0, 4095).astype(jnp.int32),
        "grad_down": bell_draw_with(key_of[7], (PARTIALS, R, D), 1.0, 6.0, ((0, 16), (2, 32)), (0, 1, 16, 2.0)),
        "grad_up": bell_draw_with(key_of[8], (PARTIALS, R, HQ), 1.0, 6.0, ((0, 16), (2, 32)), (0, 1, 16, 2.0)),
        "down_param": noise(key_of[9], (R, D), 1.0, 5.0, ((1, 32),), jnp.float32),
        "down_first": noise(key_of[10], (R, D), 0.3, 4.0, ((1, 32),), jnp.float32),
        "down_second": jnp.clip(jnp.exp(math.log(0.5) - 3.912023 * jax.random.uniform(key_of[11], (R, D), jnp.float32) ** steps_of(key_of[11], (R, D), ((1, 32),), -0.2, 0.2)), 0.01, 0.5),
        "up_param": noise(key_of[12], (R, HQ), 1.0, 5.0, ((1, 32),), jnp.float32),
        "up_first": noise(key_of[13], (R, HQ), 0.3, 4.0, ((1, 32),), jnp.float32),
        "up_second": jnp.clip(jnp.exp(math.log(0.5) - 3.912023 * jax.random.uniform(key_of[14], (R, HQ), jnp.float32) ** steps_of(key_of[14], (R, HQ), ((1, 32),), -0.2, 0.2)), 0.01, 0.5),
    }


beta_first = 0.9
beta_second = 0.999
first_fix = 0.9999734386
second_fix = 0.095207851
learn_rate = 0.5
decay_rate = 0.01
adam_eps = 1e-08
norm_eps = 1e-06
rope_base = 1000000.0

def adamw(param, first, second, grad):
    first_new = beta_first * first + (1.0 - beta_first) * grad
    second_new = beta_second * second + (1.0 - beta_second) * grad * grad
    first_hat = first_new / first_fix
    second_hat = second_new / second_fix
    return param - learn_rate * (first_hat / (jnp.sqrt(second_hat) + adam_eps) + decay_rate * param)

def rotary(query, angle):
    half = query.shape[-1] // 2
    cosine = jnp.cos(angle)
    sine = jnp.sin(angle)
    cosine = jnp.concatenate([cosine, cosine], axis=-1)
    sine = jnp.concatenate([sine, sine], axis=-1)
    turned = jnp.concatenate([-query[..., half:], query[..., :half]], axis=-1)
    return query * cosine + turned * sine

def reference(hidden_in, norm_gain, q_weight, q_gain, o_weight, kv_cache, positions, grad_down, grad_up, down_param, down_first, down_second, up_param, up_first, up_second):
    down_sum = lax.optimization_barrier(jnp.sum(grad_down.astype(jnp.float32), axis=0))
    up_sum = lax.optimization_barrier(jnp.sum(grad_up.astype(jnp.float32), axis=0))
    new_down = adamw(down_param, down_first, down_second, down_sum)
    new_up = adamw(up_param, up_first, up_second, up_sum)
    scale = 1.0 / jnp.sqrt(jnp.float32(R * D))
    delta = jnp.dot(new_down.T, new_up, precision=lax.Precision.HIGHEST, preferred_element_type=jnp.float32)
    merged = (q_weight.astype(jnp.float32) + scale * delta).astype(jnp.bfloat16)
    stream = hidden_in.astype(jnp.float32)
    inverse = lax.rsqrt(lax.optimization_barrier(jnp.mean(stream * stream, axis=-1, keepdims=True)) + norm_eps)
    normed = (stream * inverse * norm_gain).astype(jnp.bfloat16)
    query = jnp.dot(normed.reshape(STEPS * ROWS_ALL, D), merged, preferred_element_type=jnp.float32)
    query = query.reshape(STEPS, ROWS_ALL, HEADS, HEAD)
    qinv = lax.rsqrt(lax.optimization_barrier(jnp.mean(query * query, axis=-1, keepdims=True)) + norm_eps)
    query = query * qinv * q_gain
    freq = rope_base ** (-2.0 * jnp.arange(HEAD // 2, dtype=jnp.float32) / HEAD)
    angle = positions.astype(jnp.float32)[:, :, None, None] * freq
    rotated = rotary(query, angle).astype(jnp.bfloat16)
    rotated = rotated.reshape(STEPS, ROWS_ALL, KVH, HEADS // KVH, HEAD)
    keys = kv_cache[0].reshape(ROWS_ALL, CACHE, KVH, HEAD).astype(jnp.float32)
    values = kv_cache[1].reshape(ROWS_ALL, CACHE, KVH, HEAD).astype(jnp.float32)
    scores = jnp.einsum('srkgd,rckd->srkgc', rotated.astype(jnp.float32), keys) / jnp.sqrt(jnp.float32(HEAD))
    top = lax.optimization_barrier(jnp.max(scores, axis=-1, keepdims=True))
    expo = jnp.exp(scores - top)
    weights = (expo / lax.optimization_barrier(jnp.sum(expo, axis=-1, keepdims=True))).astype(jnp.bfloat16)
    heads_out = jnp.einsum('srkgc,rckd->srkgd', weights.astype(jnp.float32), values).astype(jnp.bfloat16)
    projected = jnp.dot(heads_out.reshape(STEPS * ROWS_ALL, HQ), o_weight, preferred_element_type=jnp.float32)
    decoded = (stream + projected.reshape(STEPS, ROWS_ALL, D)).astype(jnp.bfloat16)
    return (new_down, new_up, decoded)
```

```python
import jax
import jax.numpy as jnp
import numpy as np
from jax import lax
from jax.experimental import pallas as pl
from jax.experimental.pallas import tpu as pltpu
from jax.sharding import PartitionSpec as P

beta_first = 0.9
beta_second = 0.999
first_fix = 0.9999734386
second_fix = 0.095207851
learn_rate = 0.5
decay_rate = 0.01
adam_eps = 1e-08
norm_eps = 1e-06
rope_base = 1000000.0

MESH = pl.DeviceIdType.MESH
F32 = jnp.float32
BF16 = jnp.bfloat16
NZ = 16
NG = 16
FEAT = 160
WIDTH = 5120
HEAD = 128
ROWS = 128
STEPS = 4
CACHE = 8
RANK = 64
TOK = STEPS * ROWS
HQ = 4096


def adamw(param, first, second, grad):
    first_new = beta_first * first + (1.0 - beta_first) * grad
    second_new = beta_second * second + (1.0 - beta_second) * grad * grad
    first_hat = first_new / first_fix
    second_hat = second_new / second_fix
    return param - learn_rate * (first_hat / (jnp.sqrt(second_hat) + adam_eps) + decay_rate * param)


def aligned(start, size, multiple):
    return pl.ds(pl.multiple_of(start, multiple), size)


def kernel(
    hid, gain, gain_own, qw, qgain, ow, kv, pos, gdown, gup, dpar, dfir, dsec, upar, ufir, usec, freq,
    new_down, new_up, decoded,
    hidden_all, heads_all, w_raw, w_t, o_all, down_t, gd_buf, gu_buf, up_both, kv_buf, kv_f, kv_t, trig, query,
    pad_a, out_buf, local_sem, hx_s, hx_r, w_s, w_r, hcw_s, hcw_r, hcc_s, hcc_r, acw_s, acw_r, acc_s, acc_r,
    dcw_s, dcw_r, dcc_s, dcc_r, dx_s, dx_r, g_s, g_r, out_s, out_r,
):
    g = lax.axis_index("group")
    t = lax.axis_index("tensor")
    z = lax.div(t, 2)
    xh = lax.rem(t, 2)
    xo = 1 - xh
    partner = 2 * z + xo
    right = lax.rem(z + 1, NZ) * 2 + xh
    left = lax.rem(z + NZ - 1, NZ) * 2 + xh
    kvh = lax.div(t, 8)

    def zm(k):
        return lax.rem(z + 2 * NZ - k, NZ)

    def zp(k):
        return lax.rem(z + k, NZ)

    def remote(src, dst, s_sem, r_sem, axis, index):
        return pltpu.make_async_remote_copy(
            src_ref=src, dst_ref=dst, send_sem=s_sem, recv_sem=r_sem,
            device_id={axis: index}, device_id_type=MESH,
        )

    own_q = pltpu.make_async_copy(qw, w_raw.at[xh], local_sem.at[0])
    own_o = pltpu.make_async_copy(ow, o_all.at[aligned(xh * FEAT, FEAT, 32)], local_sem.at[1])
    own_kv = pltpu.make_async_copy(
        kv.at[:, aligned(xh * ROWS, ROWS, 128), :, aligned(kvh * HEAD, HEAD, 128)], kv_buf, local_sem.at[2])
    own_q.start()
    own_kv.start()
    own_o.start()

    barrier = pltpu.get_barrier_semaphore()
    for peer in (partner, right, left):
        pl.semaphore_signal(barrier, inc=1, device_id={"tensor": peer}, device_id_type=MESH)

    @pl.loop(1, NG)
    def _(k):
        pl.semaphore_signal(barrier, inc=1, device_id={"group": lax.rem(g + k, NG)}, device_id_type=MESH)

    pl.semaphore_wait(barrier, 3 + NG - 1)

    def chunk(s):
        return pl.ds(s * ROWS, ROWS)

    def hx(s):
        return remote(
            hid.at[s, :, aligned(xo * ROWS, ROWS, 128)],
            hidden_all.at[aligned(z * 2 * FEAT + xh * FEAT, FEAT, 32), chunk(s)],
            hx_s.at[s], hx_r.at[s], "tensor", partner)

    def hx_in(s):
        return remote(
            hid.at[s, :, aligned(xo * ROWS, ROWS, 128)],
            hidden_all.at[aligned(z * 2 * FEAT + xo * FEAT, FEAT, 32), chunk(s)],
            hx_s.at[s], hx_r.at[s], "tensor", partner)

    for s in range(STEPS):
        hx(s).start()

    def grad_copies(k):
        peer = lax.rem(g + k, NG)
        return (remote(gdown.at[0], gd_buf.at[k], g_s.at[0, k], g_r.at[0], "group", peer),
                remote(gup.at[0], gu_buf.at[k], g_s.at[1, k], g_r.at[1], "group", peer))

    @pl.loop(1, NG)
    def _(k):
        for copy in grad_copies(k):
            copy.start()

    for s in range(STEPS):
        hidden_all[aligned(z * 2 * FEAT + xh * FEAT, FEAT, 32), chunk(s)] = hid[s, :, aligned(xh * ROWS, ROWS, 128)]

    def ring(buf, size, k, s, forward, sems, sent):
        cw_s, cw_r, cc_s, cc_r = sems
        back = 1 if sent else 0
        if forward:
            source, s_sem, r_sem, peer = zm(k - back), cw_s.at[k - 1, s], cw_r.at[k - 1, s], right
        else:
            source, s_sem, r_sem, peer = zp(k - back), cc_s.at[k - 1, s], cc_r.at[k - 1, s], left
        block = buf.at[aligned(source * size, size, 32), chunk(s)]
        return remote(block, block, s_sem, r_sem, "tensor", peer)

    hid_sems = (hcw_s, hcw_r, hcc_s, hcc_r)
    head_sems = (acw_s, acw_r, acc_s, acc_r)

    def has(k, s, forward):
        return k < 8 or (s < 2) == forward

    def ring_step(buf, size, k, sems):
        for s in range(STEPS):
            for forward in (True, False):
                if has(k, s, forward):
                    ring(buf, size, k, s, forward, sems, False).wait_recv()
                    if k < 8 and has(k + 1, s, forward):
                        ring(buf, size, k + 1, s, forward, sems, True).start()

    def ring_end(buf, size, sems):
        for k in range(1, 9):
            for s in range(STEPS):
                for forward in (True, False):
                    if has(k, s, forward):
                        ring(buf, size, k, s, forward, sems, True).wait_send()

    for s in range(STEPS):
        hx_in(s).wait_recv()
        ring(hidden_all, 2 * FEAT, 1, s, True, hid_sems, True).start()
        ring(hidden_all, 2 * FEAT, 1, s, False, hid_sems, True).start()

    send_q = remote(qw, w_raw.at[xh], w_s.at[0], w_r.at[0], "tensor", partner)
    recv_q = remote(qw, w_raw.at[xo], w_s.at[0], w_r.at[0], "tensor", partner)
    send_o = remote(ow, o_all.at[aligned(xh * FEAT, FEAT, 32)], w_s.at[1], w_r.at[1], "tensor", partner)
    recv_o = remote(ow, o_all.at[aligned(xo * FEAT, FEAT, 32)], w_s.at[1], w_r.at[1], "tensor", partner)
    up_own = up_both.at[:, aligned(xh * HEAD, HEAD, 128)]
    up_other = up_both.at[:, aligned(xo * HEAD, HEAD, 128)]
    send_u = remote(up_own, up_own, w_s.at[2], w_r.at[2], "tensor", partner)
    recv_u = remote(up_other, up_other, w_s.at[2], w_r.at[2], "tensor", partner)
    send_q.start()
    send_o.start()

    def down_rows(zi, x):
        return down_t.at[aligned((2 * zi + x) * FEAT, FEAT, 32)]

    def down_ring(k, forward, sent):
        back = 1 if sent else 0
        if forward:
            source, sems, peer = zm(k - back), (dcw_s.at[k - 1], dcw_r.at[k - 1]), right
        else:
            source, sems, peer = zp(k - back), (dcc_s.at[k - 1], dcc_r.at[k - 1]), left
        block = down_rows(source, xh)
        return remote(block, block, *sems, "tensor", peer)

    def down_cross(j, sent):
        block = down_rows(zm(j) if j <= 8 else zp(j - 8), xh if sent else xo)
        return remote(block, block, dx_s.at[j], dx_r.at[j], "tensor", partner)

    def down_step(k):
        for forward in (True, False):
            if k < 8 or forward:
                down_ring(k, forward, False).wait_recv()
                if k < 7 or (forward and k < 8):
                    down_ring(k + 1, forward, True).start()
                down_cross(k if forward else 8 + k, True).start()

    def do_trig():
        for s in range(STEPS):
            angle = pos[s : s + 1, aligned(xh * ROWS, ROWS, 128)].astype(F32) * freq[...]
            trig[0, :, s * ROWS : (s + 1) * ROWS] = jnp.cos(angle)
            trig[1, :, s * ROWS : (s + 1) * ROWS] = jnp.sin(angle)

    def do_kv():
        own_kv.wait()
        for i in range(2):
            kv_f[...] = kv_buf[i].astype(F32)
            for c in range(CACHE):
                kv_t[i, c] = kv_f[:, c, :].T

    def do_w(x):
        @pl.loop(0, WIDTH // 128)
        def _(c):
            rows = aligned(c * 128, 128, 128)
            block = w_raw[x, rows, :].astype(F32).T * gain[pl.ds(c, 1), :]
            w_t[aligned(x * HEAD, HEAD, 128), rows] = block.astype(BF16)

    def do_adam():
        every = pl.ds(1, NG - 1)
        pltpu.make_async_copy(gd_buf.at[every], gd_buf.at[every], g_r.at[0]).wait()
        pltpu.make_async_copy(gu_buf.at[every], gu_buf.at[every], g_r.at[1]).wait()
        down_sum = gdown[0].astype(F32)
        up_sum = gup[0].astype(F32)
        for k in range(1, NG):
            down_sum += gd_buf[k].astype(F32)
            up_sum += gu_buf[k].astype(F32)
        down = adamw(dpar[...], dfir[...], dsec[...], down_sum)
        up = adamw(upar[...], ufir[...], usec[...], up_sum)
        new_down[...] = down
        new_up[...] = up
        up_both[:, aligned(xh * HEAD, HEAD, 128)] = up
        send_u.start()
        scaled = down * gain_own[...]
        hi = scaled.astype(BF16).astype(F32)
        pad_a[...] = jnp.zeros_like(pad_a)
        pad_a[:RANK, :FEAT] = hi
        pad_a[RANK:, :FEAT] = scaled - hi
        down_t[aligned((2 * z + xh) * FEAT, FEAT, 32), :] = pad_a[...].T[:FEAT, :].astype(BF16)
        down_ring(1, True, True).start()
        down_ring(1, False, True).start()
        down_cross(0, True).start()

    lag = 2
    for k in range(1, 9):
        ring_step(hidden_all, 2 * FEAT, k, hid_sems)
        if k > lag:
            down_step(k - lag)
        if k == 1:
            do_trig()
        elif k == 2:
            do_adam()
        elif k == 3:
            do_kv()
        elif k == 4:
            own_q.wait()
            do_w(xh)
        elif k == 6:
            recv_q.wait_recv()
            do_w(xo)

    def sum_squares(i, total):
        part = hidden_all[aligned(i * 64, 64, 64), :].astype(F32)
        return total + jnp.sum((part * part).reshape(8, 8, TOK), axis=0)

    square = lax.fori_loop(0, WIDTH // 64, sum_squares, jnp.zeros((8, TOK), F32))
    inverse = lax.rsqrt(jnp.sum(square, axis=0, keepdims=True) * (1.0 / WIDTH) + norm_eps)

    for k in range(9 - lag, 9):
        down_step(k)

    q_both = query.at[pl.ds(0, 2 * HEAD)]
    q_both[...] = jnp.zeros((2 * HEAD, TOK), F32)

    @pl.loop(0, WIDTH // 1024)
    def _(c):
        part = aligned(c * 1024, 1024, 1024)
        q_both[...] += jnp.dot(w_t[:, part], hidden_all[part, :], preferred_element_type=F32)

    for j in range(16):
        down_cross(j, False).wait_recv()

    def low_rank(c, total):
        part = aligned(c * 1024, 1024, 1024)
        return total + lax.dot_general(
            down_t[part, :], hidden_all[part, :], (((0,), (0,)), ((), ())), preferred_element_type=F32)

    low = lax.fori_loop(0, WIDTH // 1024, low_rank, jnp.zeros((2 * RANK, TOK), F32))
    low = low[:RANK] + low[RANK:]
    recv_u.wait_recv()
    delta = lax.dot_general(
        up_both[...], low, (((0,), (0,)), ((), ())),
        precision=lax.Precision.HIGHEST, preferred_element_type=F32)
    q_both[...] = (q_both[...] + delta * float(1.0 / np.sqrt(RANK * WIDTH))) * inverse

    qgain_col = jnp.broadcast_to(qgain[...], (HEAD, HEAD)).T
    half = HEAD // 2
    for x in range(2):
        for s in range(STEPS):
            lanes = slice(s * ROWS, (s + 1) * ROWS)
            q = query[x * HEAD : (x + 1) * HEAD, lanes]
            q = q * lax.rsqrt(jnp.sum(q * q, axis=0, keepdims=True) * (1.0 / HEAD) + norm_eps) * qgain_col
            cosine, sine = trig[0, :, lanes], trig[1, :, lanes]
            first, second = q[:half], q[half:]
            rotated = jnp.concatenate(
                [first * cosine - second * sine, second * cosine + first * sine], axis=0)
            rotated = rotated.astype(BF16).astype(F32)
            scores = jnp.concatenate(
                [jnp.sum(rotated * kv_t[0, c], axis=0, keepdims=True) for c in range(CACHE)], axis=0)
            scores = scores * float(1.0 / np.sqrt(HEAD))
            expo = jnp.exp(scores - jnp.max(scores, axis=0, keepdims=True))
            weights = (expo / jnp.sum(expo, axis=0, keepdims=True)).astype(BF16).astype(F32)
            total = weights[0:1] * kv_t[1, 0]
            for c in range(1, CACHE):
                total += weights[c : c + 1] * kv_t[1, c]
            heads_all[aligned(z * 2 * HEAD + x * HEAD, HEAD, 128), lanes] = total.astype(BF16)
    for s in range(STEPS):
        ring(heads_all, 2 * HEAD, 1, s, True, head_sems, True).start()
        ring(heads_all, 2 * HEAD, 1, s, False, head_sems, True).start()

    for k in range(1, 9):
        ring_step(heads_all, 2 * HEAD, k, head_sems)

    own_o.wait()
    recv_o.wait_recv()
    query[...] = hidden_all[aligned(z * 2 * FEAT, 2 * FEAT, 32), :].astype(F32)

    @pl.loop(0, HQ // 1024)
    def _(c):
        part = aligned(c * 1024, 1024, 1024)
        query[...] += jnp.dot(o_all[:, part], heads_all[part, :], preferred_element_type=F32)

    def out_copy(s, x):
        return remote(
            out_buf.at[s], decoded.at[s, :, aligned(x * ROWS, ROWS, 128)],
            out_s.at[s], out_r.at[s], "tensor", partner)

    for s in range(STEPS):
        lanes = slice(s * ROWS, (s + 1) * ROWS)
        out_buf[s] = query[aligned(xo * FEAT, FEAT, 32), lanes].astype(BF16)
        out_copy(s, xh).start()
        decoded[s, :, aligned(xh * ROWS, ROWS, 128)] = query[aligned(xh * FEAT, FEAT, 32), lanes].astype(BF16)

    ring_end(hidden_all, 2 * FEAT, hid_sems)
    ring_end(heads_all, 2 * HEAD, head_sems)
    for k in range(1, 9):
        down_ring(k, True, True).wait_send()
        if k < 8:
            down_ring(k, False, True).wait_send()
    for j in range(16):
        down_cross(j, True).wait_send()
    for s in range(STEPS):
        hx(s).wait_send()
    for copy in (send_q, send_o, send_u):
        copy.wait_send()

    @pl.loop(1, NG)
    def _(k):
        for copy in grad_copies(k):
            copy.wait_send()

    for s in range(STEPS):
        out_copy(s, xh).wait_send()
        out_copy(s, xo).wait_recv()


def body(hidden_in, norm_gain, q_weight, q_gain, o_weight, kv_cache, positions, grad_down, grad_up, *factors):
    t = lax.axis_index("tensor")
    freq = np.float32(rope_base) ** (-2.0 * np.arange(HEAD // 2, dtype=np.float32) / HEAD)
    freq = jnp.asarray(np.broadcast_to(freq.astype(np.float32)[:, None], (HEAD // 2, ROWS)))
    gain_own = lax.dynamic_slice(norm_gain, (t * FEAT,), (FEAT,)).reshape(1, FEAT)
    vmem = pl.BlockSpec(memory_space=pltpu.VMEM)
    anywhere = pl.BlockSpec(memory_space=pl.ANY)
    dma = pltpu.SemaphoreType.DMA
    new_down, new_up, decoded = pl.pallas_call(
        kernel,
        out_shape=(
            jax.ShapeDtypeStruct((RANK, FEAT), F32),
            jax.ShapeDtypeStruct((RANK, HEAD), F32),
            jax.ShapeDtypeStruct((STEPS, FEAT, 2 * ROWS), BF16),
        ),
        in_specs=[vmem, vmem, vmem, anywhere, vmem, anywhere, anywhere] + [vmem] * 10,
        out_specs=(vmem, vmem, vmem),
        scratch_shapes=[
            pltpu.VMEM((WIDTH, TOK), BF16),
            pltpu.VMEM((HQ, TOK), BF16),
            pltpu.VMEM((2, WIDTH, HEAD), BF16),
            pltpu.VMEM((2 * HEAD, WIDTH), BF16),
            pltpu.VMEM((2 * FEAT, HQ), BF16),
            pltpu.VMEM((WIDTH, 2 * RANK), BF16),
            pltpu.VMEM((NG, RANK, FEAT), BF16),
            pltpu.VMEM((NG, RANK, HEAD), BF16),
            pltpu.VMEM((RANK, 2 * HEAD), F32),
            pltpu.VMEM((2, ROWS, CACHE, HEAD), BF16),
            pltpu.VMEM((ROWS, CACHE, HEAD), F32),
            pltpu.VMEM((2, CACHE, HEAD, ROWS), F32),
            pltpu.VMEM((2, HEAD // 2, TOK), F32),
            pltpu.VMEM((2 * FEAT, TOK), F32),
            pltpu.VMEM((2 * RANK, 256), F32),
            pltpu.VMEM((STEPS, FEAT, ROWS), BF16),
            dma((3,)),
            dma((STEPS,)), dma((STEPS,)),
            dma((3,)), dma((3,)),
            dma((8, STEPS)), dma((8, STEPS)), dma((8, STEPS)), dma((8, STEPS)),
            dma((8, STEPS)), dma((8, STEPS)), dma((8, STEPS)), dma((8, STEPS)),
            dma((8,)), dma((8,)), dma((8,)), dma((8,)),
            dma((16,)), dma((16,)),
            dma((2, NG)), dma((2,)),
            dma((STEPS,)), dma((STEPS,)),
        ],
        compiler_params=pltpu.CompilerParams(
            collective_id=0, has_side_effects=True, vmem_limit_bytes=56 * 1024 * 1024),
        cost_estimate=pl.CostEstimate(flops=3_000_000_000, bytes_accessed=10_000_000, transcendentals=100_000),
    )(
        jnp.transpose(hidden_in, (0, 2, 1)), norm_gain.reshape(WIDTH // 128, 128), gain_own, q_weight,
        q_gain.reshape(1, HEAD), jnp.transpose(o_weight), kv_cache, positions, grad_down, grad_up,
        *factors, freq,
    )
    return new_down, new_up, jnp.transpose(decoded, (0, 2, 1))


def solution(mesh):
    in_specs = (
        P(None, "group", "tensor"),
        P(),
        P(None, "tensor"),
        P(),
        P(None, "tensor"),
        P(None, "group", None, None),
        P(None, "group"),
        P("group", None, "tensor"),
        P("group", None, "tensor"),
        P(None, "tensor"),
        P(None, "tensor"),
        P(None, "tensor"),
        P(None, "tensor"),
        P(None, "tensor"),
        P(None, "tensor"),
    )
    out_specs = (P(None, "tensor"), P(None, "tensor"), P(None, "group", "tensor"))
    return jax.shard_map(body, mesh=mesh, in_specs=in_specs, out_specs=out_specs, check_vma=False)
```

```python
import jax
import jax.numpy as jnp
import numpy as np
from jax import lax
from jax.experimental import pallas as pl
from jax.experimental.pallas import tpu as pltpu
from jax.sharding import PartitionSpec as P

beta_first = 0.9
beta_second = 0.999
first_fix = 0.9999734386
second_fix = 0.095207851
learn_rate = 0.5
decay_rate = 0.01
adam_eps = 1e-08
norm_eps = 1e-06
rope_base = 1000000.0

MESH = pl.DeviceIdType.MESH
F32 = jnp.float32
BF16 = jnp.bfloat16
NZ = 16
NG = 16
FEAT = 160
WIDTH = 5120
HEAD = 128
ROWS = 128
STEPS = 4
CACHE = 8
RANK = 64
TOK = STEPS * ROWS
HQ = 4096


def adamw(param, first, second, grad):
    first_new = beta_first * first + (1.0 - beta_first) * grad
    second_new = beta_second * second + (1.0 - beta_second) * grad * grad
    first_hat = first_new / first_fix
    second_hat = second_new / second_fix
    return param - learn_rate * (first_hat / (jnp.sqrt(second_hat) + adam_eps) + decay_rate * param)


def aligned(start, size, multiple):
    return pl.ds(pl.multiple_of(start, multiple), size)


def kernel(
    hid, gain, qw, qgain, ow, kv, pos, gdown, gup, dpar, dfir, dsec, upar, ufir, usec, freq_hbm,
    new_down, new_up, decoded,
    hidden_all, heads_all, w_raw, o_all, down_t, gd_buf, gu_buf, up_both, kv_buf, kv_f, kv_t, trig, query, low,
    square, gain_col, freq, pad_a, out_buf,
    local_sem, hx_s, hx_r, w_s, w_r, hcw_s, hcw_r, hcc_s, hcc_r, acw_s, acw_r, acc_s, acc_r,
    da_s, da_r, dx_s, dx_r, db_s, db_r, g_s, g_r, out_s, out_r,
):
    g = lax.axis_index("group")
    t = lax.axis_index("tensor")
    z = lax.div(t, 2)
    xh = lax.rem(t, 2)
    xo = 1 - xh
    core = lax.rem(g, 2)
    sibling = g + 1 - 2 * core
    partner = 2 * z + xo
    right = lax.rem(z + 1, NZ) * 2 + xh
    left = lax.rem(z + NZ - 1, NZ) * 2 + xh
    kvh = lax.div(t, 8)

    def zm(k):
        return lax.rem(z + 2 * NZ - k, NZ)

    def zp(k):
        return lax.rem(z + k, NZ)

    def remote(src, dst, s_sem, r_sem, axis, index):
        return pltpu.make_async_remote_copy(
            src_ref=src, dst_ref=dst, send_sem=s_sem, recv_sem=r_sem,
            device_id={axis: index}, device_id_type=MESH,
        )

    def lanes(s):
        return pl.ds(s * ROWS, ROWS)

    own_q = pltpu.make_async_copy(qw, w_raw.at[xh], local_sem.at[0])
    own_o = pltpu.make_async_copy(ow, o_all.at[aligned(xh * FEAT, FEAT, 32)], local_sem.at[1])
    own_kv = pltpu.make_async_copy(
        kv.at[:, aligned(xh * ROWS, ROWS, 128), :, aligned(kvh * HEAD, HEAD, 128)], kv_buf, local_sem.at[2])
    own_freq = pltpu.make_async_copy(freq_hbm, freq, local_sem.at[3])
    own_freq.start()
    own_kv.start()
    own_q.start()
    own_o.start()

    barrier = pltpu.get_barrier_semaphore()
    pl.semaphore_signal(barrier, inc=1, device_id={"tensor": partner}, device_id_type=MESH)

    @pl.loop(1, NG)
    def _(k):
        pl.semaphore_signal(barrier, inc=1, device_id={"tensor": 2 * zp(k) + xh}, device_id_type=MESH)
        pl.semaphore_signal(barrier, inc=1, device_id={"group": lax.rem(g + k, NG)}, device_id_type=MESH)

    for s in range(STEPS):
        hidden_all[aligned((2 * z + xh) * FEAT, FEAT, 32), lanes(s)] = hid[s, :, aligned(xh * ROWS, ROWS, 128)]

    pl.semaphore_wait(barrier, 1 + 2 * (NG - 1))

    def hx(s, sent):
        return remote(
            hid.at[s, :, aligned(xo * ROWS, ROWS, 128)],
            hidden_all.at[aligned((2 * z + (xh if sent else xo)) * FEAT, FEAT, 32), lanes(s)],
            hx_s.at[s], hx_r.at[s], "tensor", partner)

    def hidden_chunk(zi, j):
        x = xh if j < 2 else xo
        return hidden_all.at[aligned((2 * zi + x) * FEAT, FEAT, 32), pl.ds((j % 2) * 2 * ROWS, 2 * ROWS)]

    def head_chunk(zi, j):
        return heads_all.at[aligned(zi * 2 * HEAD, 2 * HEAD, 256), lanes(j)]

    def ring(chunk, k, j, forward, sems, sent):
        cw_s, cw_r, cc_s, cc_r = sems
        back = 1 if sent else 0
        if forward:
            source, s_sem, r_sem, peer = zm(k - back), cw_s.at[k - 1, j], cw_r.at[k - 1, j], right
        else:
            source, s_sem, r_sem, peer = zp(k - back), cc_s.at[k - 1, j], cc_r.at[k - 1, j], left
        block = chunk(source, j)
        return remote(block, block, s_sem, r_sem, "tensor", peer)

    hid_sems = (hcw_s, hcw_r, hcc_s, hcc_r)
    head_sems = (acw_s, acw_r, acc_s, acc_r)

    def has(k, j, forward):
        return k < 8 or (j % 2 == 0) == forward

    def ring_start(chunk, j, sems):
        ring(chunk, 1, j, True, sems, True).start()
        ring(chunk, 1, j, False, sems, True).start()

    def ring_run(chunk, sems, work):
        for k in range(1, 9):
            for j in range(4):
                for forward in (True, False):
                    if has(k, j, forward):
                        ring(chunk, k, j, forward, sems, False).wait_recv()
                        if k < 8 and has(k + 1, j, forward):
                            ring(chunk, k + 1, j, forward, sems, True).start()
                for unit in work.get((k, j), ()):
                    unit()

    def ring_end(chunk, sems):
        for k in range(1, 9):
            for j in range(4):
                for forward in (True, False):
                    if has(k, j, forward):
                        ring(chunk, k, j, forward, sems, True).wait_send()

    def grad_copies(k):
        peer = lax.rem(g + k, NG)
        return (remote(gdown.at[0], gd_buf.at[k], g_s.at[0, k], g_r.at[0], "group", peer),
                remote(gup.at[0], gu_buf.at[k], g_s.at[1, k], g_r.at[1], "group", peer))

    for s in range(STEPS):
        hx(s, True).start()
    ring_start(hidden_chunk, 0, hid_sems)
    ring_start(hidden_chunk, 1, hid_sems)

    @pl.loop(1, NG)
    def _(k):
        for copy in grad_copies(k):
            copy.start()

    def q_half(x, c):
        return w_raw.at[x, aligned(c * (WIDTH // 2), WIDTH // 2, 32)]

    def o_half(x, c):
        return o_all.at[aligned(x * FEAT, FEAT, 32), aligned(c * (HQ // 2), HQ // 2, 128)]

    def send_q(sent):
        return remote(qw.at[aligned(core * (WIDTH // 2), WIDTH // 2, 32)], q_half(xh if sent else xo, core),
                      w_s.at[0], w_r.at[0], "tensor", partner)

    def share_q(sent):
        return remote(q_half(xo, core), q_half(xo, core if sent else 1 - core),
                      w_s.at[1], w_r.at[1], "group", sibling)

    def send_o(sent):
        return remote(ow.at[:, aligned(core * (HQ // 2), HQ // 2, 128)], o_half(xh if sent else xo, core),
                      w_s.at[2], w_r.at[2], "tensor", partner)

    def share_o(sent):
        return remote(o_half(xo, core), o_half(xo, core if sent else 1 - core),
                      w_s.at[3], w_r.at[3], "group", sibling)

    def send_u(sent):
        block = up_both.at[:, aligned((xh if sent else xo) * HEAD, HEAD, 128)]
        return remote(block, block, w_s.at[4], w_r.at[4], "tensor", partner)

    send_q(True).start()
    for s in range(STEPS):
        hx(s, False).wait_recv()
        if s % 2:
            ring_start(hidden_chunk, 2 + s // 2, hid_sems)

    def down_rows(zi, x):
        return down_t.at[aligned((2 * zi + x) * FEAT, FEAT, 32)]

    def down_along(k):
        return remote(down_rows(g, xh), down_rows(g, xh), da_s.at[k], da_r.at[0], "tensor", 2 * zp(k) + xh)

    def down_cross(sent):
        block = down_rows(g, xh if sent else xo)
        return remote(block, block, dx_s.at[0], dx_r.at[0], "tensor", partner)

    def down_share(k, sent):
        owner = g if sent else lax.rem(g + NG - k, NG)
        block = down_t.at[aligned(owner * 2 * FEAT, 2 * FEAT, 32)]
        return remote(block, block, db_s.at[k], db_r.at[k], "group", lax.rem(g + k, NG))

    def down_first_part():
        @pl.when(z != g)
        def _():
            down_along(1).wait_recv()

        down_cross(True).start()

    def down_second_part():
        down_cross(False).wait_recv()

        @pl.loop(1, NG)
        def _(k):
            down_share(k, True).start()

    def down_wait():
        @pl.loop(1, NG)
        def _(k):
            down_share(k, False).wait_recv()

    def do_gain(i):
        for c in range(8 * i, 8 * i + 8):
            gain_col[c * 128 : (c + 1) * 128, :] = jnp.broadcast_to(gain[c : c + 1, :], (128, 128)).T

    def do_trig(s):
        angle = pos[s : s + 1, aligned(xh * ROWS, ROWS, 128)].astype(F32) * freq[...]
        trig[0, :, lanes(s)] = jnp.cos(angle)
        trig[1, :, lanes(s)] = jnp.sin(angle)

    def do_kv(i, j):
        if j == 0:
            kv_f[...] = kv_buf[i].astype(F32)
        for c in range(4 * j, 4 * j + 4):
            kv_t[i, c] = kv_f[:, c, :].T

    def do_w(x, i):
        part = pl.ds(i * 1024, 1024)
        w_raw[x, part, :] = (w_raw[x, part, :].astype(F32) * gain_col[part, :]).astype(BF16)

    def do_sums():
        every = pl.ds(1, NG - 1)
        pltpu.make_async_copy(gd_buf.at[every], gd_buf.at[every], g_r.at[0]).wait()
        pltpu.make_async_copy(gu_buf.at[every], gu_buf.at[every], g_r.at[1]).wait()
        down_sum = gdown[0].astype(F32)
        up_sum = gup[0].astype(F32)
        for k in range(1, NG):
            down_sum += gd_buf[k].astype(F32)
            up_sum += gu_buf[k].astype(F32)
        down = adamw(dpar[...], dfir[...], dsec[...], down_sum)
        up = adamw(upar[...], ufir[...], usec[...], up_sum)
        new_down[...] = down
        new_up[...] = up
        up_both[:, aligned(xh * HEAD, HEAD, 128)] = up
        send_u(True).start()

        @pl.when(z == g)
        def _():
            pad_a[...] = jnp.zeros_like(pad_a)
            pad_a[:RANK, :FEAT] = down
            pad_a[RANK:, :FEAT] = down
            scaled = pad_a[...].T[:FEAT, :] * gain_col[aligned(t * FEAT, FEAT, 32), :]
            hi = scaled.astype(BF16).astype(F32)
            lane = lax.broadcasted_iota(jnp.int32, (FEAT, 2 * RANK), 1)
            down_t[aligned((2 * g + xh) * FEAT, FEAT, 32), :] = jnp.where(lane < RANK, hi, scaled - hi).astype(BF16)

            @pl.loop(1, NZ)
            def _(k):
                down_along(k).start()

    q_both = query.at[pl.ds(0, 2 * HEAD)]
    across = (((0,), (0,)), ((), ()))

    def q_block(zi):
        rows = aligned(zi * 2 * FEAT, 2 * FEAT, 64)
        block = hidden_all[rows, :]
        for x in range(2):
            query[x * HEAD : (x + 1) * HEAD, :] += lax.dot_general(
                w_raw[x, rows, :], block, across, preferred_element_type=F32)
        wide = block.astype(F32)
        square[...] += jnp.sum((wide * wide).reshape(2 * FEAT // 8, 8, TOK), axis=0)

    def low_block(zi):
        rows = aligned(zi * 2 * FEAT, 2 * FEAT, 64)
        low[...] += lax.dot_general(down_t[rows, :], hidden_all[rows, :], across, preferred_element_type=F32)

    def start_sums():
        q_both[...] = jnp.zeros((2 * HEAD, TOK), F32)
        low[...] = jnp.zeros_like(low)
        square[...] = jnp.zeros_like(square)

    arrived = [zm(0)] + [f(k) for k in range(1, 8) for f in (zm, zp)]
    work = {
        (1, 0): [lambda: do_gain(0), lambda: do_gain(1)],
        (1, 1): [lambda: do_gain(2), lambda: do_gain(3)],
        (1, 2): [lambda: do_gain(4), own_freq.wait, lambda: do_trig(0)],
        (1, 3): [lambda: do_trig(1)],
        (2, 0): [do_sums],
        (2, 1): [lambda: do_trig(2)],
        (2, 2): [lambda: do_trig(3)],
        (2, 3): [own_kv.wait, lambda: do_kv(0, 0)],
        (3, 0): [lambda: do_kv(0, 1)],
        (3, 1): [lambda: do_kv(1, 0)],
        (3, 2): [lambda: do_kv(1, 1)],
        (3, 3): [own_q.wait, lambda: do_w(xh, 0)],
        (4, 0): [down_first_part, lambda: do_w(xh, 1)],
        (4, 1): [send_q(False).wait_recv, share_q(True).start],
        (4, 2): [lambda: do_w(xh, 2), lambda: do_w(xh, 3)],
        (4, 3): [lambda: do_w(xh, 4), start_sums],
        (5, 0): [down_second_part, send_o(True).start],
        (5, 1): [share_q(False).wait_recv, share_q(True).wait_send, lambda: do_w(xo, 0)],
        (5, 2): [lambda: do_w(xo, 1), lambda: do_w(xo, 2)],
        (5, 3): [lambda: do_w(xo, 3), lambda: do_w(xo, 4)],
    }
    for i in range(8):
        work.setdefault((6, i // 2), []).append(lambda zi=arrived[i]: q_block(zi))
    for i in range(8, 13):
        work.setdefault((7, min(i - 8, 3)), []).append(lambda zi=arrived[i]: q_block(zi))
    work[(8, 0)] = [lambda zi=arrived[13]: q_block(zi), lambda zi=arrived[14]: q_block(zi)]
    work[(8, 1)] = [down_wait] + [lambda zi=zi: low_block(zi) for zi in arrived[:5]]
    work[(8, 2)] = [lambda zi=zi: low_block(zi) for zi in arrived[5:10]]
    ring_run(hidden_chunk, hid_sems, work)
    for zi in arrived[10:] + [zm(8)]:
        low_block(zi)
    q_block(zm(8))

    inverse = lax.rsqrt(jnp.sum(square[...], axis=0, keepdims=True) * (1.0 / WIDTH) + norm_eps)
    send_u(False).wait_recv()
    delta = lax.dot_general(
        up_both[...], low[:RANK, :] + low[RANK:, :], across,
        precision=lax.Precision.HIGHEST, preferred_element_type=F32)
    q_both[...] = (q_both[...] + delta * float(1.0 / np.sqrt(RANK * WIDTH))) * inverse

    qgain_col = jnp.broadcast_to(qgain[...], (HEAD, HEAD)).T
    half = HEAD // 2
    for s in range(STEPS):
        for x in range(2):
            q = query[x * HEAD : (x + 1) * HEAD, lanes(s)]
            q = q * lax.rsqrt(jnp.sum(q * q, axis=0, keepdims=True) * (1.0 / HEAD) + norm_eps) * qgain_col
            cosine, sine = trig[0, :, lanes(s)], trig[1, :, lanes(s)]
            first, second = q[:half], q[half:]
            rotated = jnp.concatenate(
                [first * cosine - second * sine, second * cosine + first * sine], axis=0)
            rotated = rotated.astype(BF16).astype(F32)
            scores = jnp.concatenate(
                [jnp.sum(rotated * kv_t[0, c], axis=0, keepdims=True) for c in range(CACHE)], axis=0)
            scores = scores * float(1.0 / np.sqrt(HEAD))
            expo = jnp.exp(scores - jnp.max(scores, axis=0, keepdims=True))
            weights = (expo / jnp.sum(expo, axis=0, keepdims=True)).astype(BF16).astype(F32)
            total = weights[0:1] * kv_t[1, 0]
            for c in range(1, CACHE):
                total += weights[c : c + 1] * kv_t[1, c]
            heads_all[aligned((2 * z + x) * HEAD, HEAD, 128), lanes(s)] = total.astype(BF16)
        ring_start(head_chunk, s, head_sems)

    def o_start():
        query[...] = hidden_all[aligned(z * 2 * FEAT, 2 * FEAT, 64), :].astype(F32)

    def o_block(zi):
        part = aligned(zi * 2 * HEAD, 2 * HEAD, 256)
        query[...] += jnp.dot(o_all[:, part], heads_all[part, :], preferred_element_type=F32)

    work = {
        (1, 0): [send_o(False).wait_recv, share_o(True).start],
        (1, 1): [o_start],
        (1, 3): [own_o.wait, share_o(False).wait_recv],
        (2, 3): [lambda: o_block(zm(0))],
    }
    for k in range(2, 9):
        work.setdefault((k, 0), []).append(lambda k=k: o_block(zm(k - 1)))
        work.setdefault((k, 1), []).append(lambda k=k: o_block(zp(k - 1)))
    ring_run(head_chunk, head_sems, work)
    o_block(zm(8))

    def out_copy(s, x):
        return remote(
            out_buf.at[s], decoded.at[s, :, aligned(x * ROWS, ROWS, 128)],
            out_s.at[s], out_r.at[s], "tensor", partner)

    for s in range(STEPS):
        out_buf[s] = query[aligned(xo * FEAT, FEAT, 32), lanes(s)].astype(BF16)
        out_copy(s, xh).start()
    for s in range(STEPS):
        decoded[s, :, aligned(xh * ROWS, ROWS, 128)] = query[aligned(xh * FEAT, FEAT, 32), lanes(s)].astype(BF16)

    ring_end(hidden_chunk, hid_sems)
    ring_end(head_chunk, head_sems)
    for s in range(STEPS):
        hx(s, True).wait_send()
    for copy in (send_q, send_o, share_o, send_u, down_cross):
        copy(True).wait_send()

    @pl.when(z == g)
    def _():
        @pl.loop(1, NZ)
        def _(k):
            down_along(k).wait_send()

    @pl.loop(1, NG)
    def _(k):
        for copy in grad_copies(k):
            copy.wait_send()
        down_share(k, True).wait_send()

    for s in range(STEPS):
        out_copy(s, xh).wait_send()
        out_copy(s, xo).wait_recv()


def body(hidden_in, norm_gain, q_weight, q_gain, o_weight, kv_cache, positions, grad_down, grad_up, *factors):
    freq = np.float32(rope_base) ** (-2.0 * np.arange(HEAD // 2, dtype=np.float32) / HEAD)
    freq = jnp.asarray(np.broadcast_to(freq.astype(np.float32)[:, None], (HEAD // 2, ROWS)))
    vmem = pl.BlockSpec(memory_space=pltpu.VMEM)
    anywhere = pl.BlockSpec(memory_space=pl.ANY)
    dma = pltpu.SemaphoreType.DMA
    new_down, new_up, decoded = pl.pallas_call(
        kernel,
        out_shape=(
            jax.ShapeDtypeStruct((RANK, FEAT), F32),
            jax.ShapeDtypeStruct((RANK, HEAD), F32),
            jax.ShapeDtypeStruct((STEPS, FEAT, 2 * ROWS), BF16),
        ),
        in_specs=[vmem, vmem, anywhere, vmem, anywhere, anywhere] + [vmem] * 9 + [anywhere],
        out_specs=(vmem, vmem, vmem),
        scratch_shapes=[
            pltpu.VMEM((WIDTH, TOK), BF16),
            pltpu.VMEM((HQ, TOK), BF16),
            pltpu.VMEM((2, WIDTH, HEAD), BF16),
            pltpu.VMEM((2 * FEAT, HQ), BF16),
            pltpu.VMEM((WIDTH, 2 * RANK), BF16),
            pltpu.VMEM((NG, RANK, FEAT), BF16),
            pltpu.VMEM((NG, RANK, HEAD), BF16),
            pltpu.VMEM((RANK, 2 * HEAD), F32),
            pltpu.VMEM((2, ROWS, CACHE, HEAD), BF16),
            pltpu.VMEM((ROWS, CACHE, HEAD), F32),
            pltpu.VMEM((2, CACHE, HEAD, ROWS), F32),
            pltpu.VMEM((2, HEAD // 2, TOK), F32),
            pltpu.VMEM((2 * FEAT, TOK), F32),
            pltpu.VMEM((2 * RANK, TOK), F32),
            pltpu.VMEM((8, TOK), F32),
            pltpu.VMEM((WIDTH, 128), F32),
            pltpu.VMEM((HEAD // 2, ROWS), F32),
            pltpu.VMEM((2 * RANK, 256), F32),
            pltpu.VMEM((STEPS, FEAT, ROWS), BF16),
            dma((4,)),
            dma((STEPS,)), dma((STEPS,)),
            dma((5,)), dma((5,)),
            dma((8, 4)), dma((8, 4)), dma((8, 4)), dma((8, 4)),
            dma((8, 4)), dma((8, 4)), dma((8, 4)), dma((8, 4)),
            dma((NZ,)), dma((1,)), dma((1,)), dma((1,)), dma((NG,)), dma((NG,)),
            dma((2, NG)), dma((2,)),
            dma((STEPS,)), dma((STEPS,)),
        ],
        compiler_params=pltpu.CompilerParams(
            collective_id=0, has_side_effects=True, vmem_limit_bytes=56 * 1024 * 1024),
        cost_estimate=pl.CostEstimate(flops=3_000_000_000, bytes_accessed=10_000_000, transcendentals=100_000),
    )(
        jnp.transpose(hidden_in, (0, 2, 1)), norm_gain.reshape(WIDTH // 128, 128), q_weight,
        q_gain.reshape(1, HEAD), jnp.transpose(o_weight), kv_cache, positions, grad_down, grad_up,
        *factors, freq,
    )
    return new_down, new_up, jnp.transpose(decoded, (0, 2, 1))


def solution(mesh):
    in_specs = (
        P(None, "group", "tensor"),
        P(),
        P(None, "tensor"),
        P(),
        P(None, "tensor"),
        P(None, "group", None, None),
        P(None, "group"),
        P("group", None, "tensor"),
        P("group", None, "tensor"),
        P(None, "tensor"),
        P(None, "tensor"),
        P(None, "tensor"),
        P(None, "tensor"),
        P(None, "tensor"),
        P(None, "tensor"),
    )
    out_specs = (P(None, "tensor"), P(None, "tensor"), P(None, "group", "tensor"))
    return jax.shard_map(body, mesh=mesh, in_specs=in_specs, out_specs=out_specs, check_vma=False)
```

```python
import jax
import jax.numpy as jnp
import numpy as np
from jax import lax
from jax.experimental import pallas as pl
from jax.experimental.pallas import tpu as pltpu
from jax.sharding import PartitionSpec as P

beta_first = 0.9
beta_second = 0.999
first_fix = 0.9999734386
second_fix = 0.095207851
learn_rate = 0.5
decay_rate = 0.01
adam_eps = 1e-08
norm_eps = 1e-06
rope_base = 1000000.0

MESH = pl.DeviceIdType.MESH
F32 = jnp.float32
BF16 = jnp.bfloat16
NZ = 16
NG = 16
FEAT = 160
WIDTH = 5120
HEAD = 128
ROWS = 128
STEPS = 4
CACHE = 8
RANK = 64
TOK = STEPS * ROWS
HQ = 4096
PIECES = 16


def adamw(param, first, second, grad):
    first_new = beta_first * first + (1.0 - beta_first) * grad
    second_new = beta_second * second + (1.0 - beta_second) * grad * grad
    first_hat = first_new / first_fix
    second_hat = second_new / second_fix
    return param - learn_rate * (first_hat / (jnp.sqrt(second_hat) + adam_eps) + decay_rate * param)


def aligned(start, size, multiple):
    return pl.ds(pl.multiple_of(start, multiple), size)


def kernel(
    hid, gain_h, qw, qgain_h, ow, kv, pos_h, gdown, gup, dpar_h, dfir_h, dsec_h, upar_h, ufir_h, usec_h,
    new_down, new_up, decoded,
    hidden_all, heads_all, w_raw, o_all, down_t, gd_buf, gu_buf, up_both, kv_buf, kv_f, kv_t, trig, query, low,
    square, result, gain_col, pad_a, out_buf,
    gain, qgain, pos, dpar, dfir, dsec, upar, ufir, usec,
    local_sem, hx_s, hx_r, w_s, w_r, cw_s, cw_r, cc_s, cc_r,
    da_s, da_r, dx_s, dx_r, db_s, db_r, dc_s, dc_r, g_s, g_r, out_s, out_r,
):
    g = lax.axis_index("group")
    t = lax.axis_index("tensor")
    z = lax.div(t, 2)
    xh = lax.rem(t, 2)
    xo = 1 - xh
    core = lax.rem(g, 2)
    sibling = g + 1 - 2 * core
    partner = 2 * z + xo
    right = lax.rem(z + 1, NZ) * 2 + xh
    left = lax.rem(z + NZ - 1, NZ) * 2 + xh
    kvh = lax.div(t, 8)
    beside = {"group": lax.rem(g + NG // 2, NG), "tensor": partner}

    def zm(k):
        return lax.rem(z + 2 * NZ - k, NZ)

    def zp(k):
        return lax.rem(z + k, NZ)

    def remote(src, dst, s_sem, r_sem, device):
        return pltpu.make_async_remote_copy(
            src_ref=src, dst_ref=dst, send_sem=s_sem, recv_sem=r_sem, device_id=device, device_id_type=MESH)

    def lanes(s):
        return pl.ds(s * ROWS, ROWS)

    def lanes_half(h):
        return pl.ds(h * 2 * ROWS, 2 * ROWS)

    barrier = pltpu.get_barrier_semaphore()
    pl.semaphore_signal(barrier, inc=1, device_id={"tensor": partner}, device_id_type=MESH)
    pl.semaphore_signal(barrier, inc=1, device_id=beside, device_id_type=MESH)

    @pl.loop(1, NG)
    def _(k):
        pl.semaphore_signal(barrier, inc=1, device_id={"tensor": 2 * zp(k) + xh}, device_id_type=MESH)
        pl.semaphore_signal(barrier, inc=1, device_id={"group": lax.rem(g + k, NG)}, device_id_type=MESH)

    def own_hidden(s):
        return pltpu.make_async_copy(
            hid.at[s, :, aligned(xh * ROWS, ROWS, 128)],
            hidden_all.at[aligned((2 * z + xh) * FEAT, FEAT, 32), lanes(s)], local_sem.at[s])

    small = [pltpu.make_async_copy(a, b, local_sem.at[4 + i]) for i, (a, b) in enumerate((
        (gain_h, gain), (qgain_h, qgain), (pos_h, pos), (dpar_h, dpar), (dfir_h, dfir), (dsec_h, dsec),
        (upar_h, upar), (ufir_h, ufir), (usec_h, usec)))]
    own_grads = (pltpu.make_async_copy(gdown.at[0], gd_buf.at[0], local_sem.at[13]),
                 pltpu.make_async_copy(gup.at[0], gu_buf.at[0], local_sem.at[14]))
    own_kv = pltpu.make_async_copy(
        kv.at[:, aligned(xh * ROWS, ROWS, 128), :, aligned(kvh * HEAD, HEAD, 128)], kv_buf, local_sem.at[15])
    own_q = pltpu.make_async_copy(qw, w_raw.at[xh], local_sem.at[16])
    own_o = pltpu.make_async_copy(ow, o_all.at[aligned(xh * FEAT, FEAT, 32)], local_sem.at[17])
    for s in range(STEPS):
        own_hidden(s).start()
    for copy in small:
        copy.start()
    for copy in own_grads:
        copy.start()
    own_kv.start()
    own_q.start()
    own_o.start()
    for s in range(STEPS):
        own_hidden(s).wait()

    pl.semaphore_wait(barrier, 2 + 2 * (NG - 1))

    def hx(s, sent):
        return remote(
            hid.at[s, :, aligned(xo * ROWS, ROWS, 128)],
            hidden_all.at[aligned((2 * z + (xh if sent else xo)) * FEAT, FEAT, 32), lanes(s)],
            hx_s.at[s], hx_r.at[s], {"tensor": partner})

    def chunk(phase, zi, j):
        if phase == 0:
            x = xh if j < 2 else xo
            return hidden_all.at[aligned((2 * zi + x) * FEAT, FEAT, 32), lanes_half(j % 2)]
        return heads_all.at[aligned(zi * 2 * HEAD, 2 * HEAD, 256), lanes(j)]

    def ring(phase, k, j, forward, sent):
        back = 1 if sent else 0
        at = phase, k - 1, j
        if forward:
            source, s_sem, r_sem, peer = zm(k - back), cw_s.at[at], cw_r.at[at], right
        else:
            source, s_sem, r_sem, peer = zp(k - back), cc_s.at[at], cc_r.at[at], left
        block = chunk(phase, source, j)
        return remote(block, block, s_sem, r_sem, {"tensor": peer})

    def has(k, j, forward):
        return k < 8 or (j % 2 == 0) == forward

    def ring_start(phase, *which):
        for j in which:
            ring(phase, 1, j, True, True).start()
            ring(phase, 1, j, False, True).start()

    def ring_step(phase, k, j):
        for forward in (True, False):
            if has(k, j, forward):
                ring(phase, k, j, forward, False).wait_recv()
                if k < 8 and has(k + 1, j, forward):
                    ring(phase, k + 1, j, forward, True).start()

    def ring_run(phase, work):
        steps = [(k, j) for k in range(1, 9) for j in range(4)]
        if phase == 0:
            steps = [(1, 0), (1, 1)]
            for k in range(1, 8):
                steps += [(k + 1, 0), (k + 1, 1), (k, 2), (k, 3)]
            steps += [(8, 2), (8, 3)]
        for slot, (k, j) in enumerate(steps):
            ring_step(phase, k, j)
            if phase == 0:
                if slot == 1:
                    start_other()
                for i in range(PIECES):
                    if i * 12 // PIECES == slot:
                        q_piece(i)
                    if i + 12 == slot:
                        o_piece(i)
            for unit in work.get((slot // 4 + 1, slot % 4), ()):
                unit()

    def ring_end(phase):
        for k in range(1, 9):
            for j in range(4):
                for forward in (True, False):
                    if has(k, j, forward):
                        ring(phase, k, j, forward, True).wait_send()

    def grad_copies(k):
        peer = {"group": lax.rem(g + k, NG)}
        return (remote(gdown.at[0], gd_buf.at[k], g_s.at[0, k], g_r.at[0], peer),
                remote(gup.at[0], gu_buf.at[k], g_s.at[1, k], g_r.at[1], peer))

    for s in range(STEPS):
        hx(s, True).start()
    ring_start(0, 0, 1)

    def send_grads(first, last):
        def run():
            @pl.loop(first, last)
            def _(k):
                for copy in grad_copies(k):
                    copy.start()

        return run

    send_grads(1, 5)()

    def q_half(x, c):
        return w_raw.at[x, aligned(c * (WIDTH // 2), WIDTH // 2, 32)]

    def o_half(x, c):
        return o_all.at[aligned(x * FEAT, FEAT, 32), aligned(c * (HQ // 2), HQ // 2, 128)]

    def send_q(sent):
        return remote(qw.at[aligned(core * (WIDTH // 2), WIDTH // 2, 32)], q_half(xh if sent else xo, core),
                      w_s.at[0], w_r.at[0], beside)

    def q_piece(i):
        rows = aligned(core * (WIDTH // 2) + i * FEAT, FEAT, 32)
        remote(qw.at[rows], w_raw.at[xh, rows], w_s.at[0], w_r.at[0], beside).start()

    def o_piece(i):
        part = aligned(core * (HQ // 2) + i * 128, 128, 128)
        remote(ow.at[:, part], o_all.at[aligned(xh * FEAT, FEAT, 32), part], w_s.at[2], w_r.at[2], beside).start()

    def share_q(sent):
        return remote(q_half(xo, core), q_half(xo, core if sent else 1 - core),
                      w_s.at[1], w_r.at[1], {"group": sibling})

    def send_o(sent):
        return remote(ow.at[:, aligned(core * (HQ // 2), HQ // 2, 128)], o_half(xh if sent else xo, core),
                      w_s.at[2], w_r.at[2], beside)

    def share_o(sent):
        return remote(o_half(xo, core), o_half(xo, core if sent else 1 - core),
                      w_s.at[3], w_r.at[3], {"group": sibling})

    def send_u(sent):
        block = up_both.at[:, aligned((xh if sent else xo) * HEAD, HEAD, 128)]
        return remote(block, block, w_s.at[4], w_r.at[4], {"tensor": partner})


    def down_rows(zi, x):
        return down_t.at[aligned((2 * zi + x) * FEAT, FEAT, 32)]

    def down_pair(zi):
        return down_t.at[aligned(zi * 2 * FEAT, 2 * FEAT, 64)]

    def down_along(k):
        return remote(down_rows(g, xh), down_rows(g, xh), da_s.at[k], da_r.at[0], {"tensor": 2 * zp(k) + xh})

    def down_cross(sent):
        block = down_rows(g, xh if sent else xo)
        return remote(block, block, dx_s.at[0], dx_r.at[0], {"tensor": partner})

    def down_share(k, sent):
        block = down_pair(g if sent else lax.rem(g + NG - 2 * k, NG))
        return remote(block, block, db_s.at[k], db_r.at[k], {"group": lax.rem(g + 2 * k, NG)})

    def down_pass(k, sent):
        block = down_pair(lax.rem((g if sent else sibling) + NG - 2 * k, NG))
        return remote(block, block, dc_s.at[k], dc_r.at[k], {"group": sibling})

    def down_first_part():
        @pl.when(z != g)
        def _():
            down_along(1).wait_recv()

        down_cross(True).start()

    def down_second_part():
        down_cross(False).wait_recv()

        down_share(1, True).start()

    def down_third_part():
        @pl.loop(1, NG // 2)
        def _(k):
            down_share(k, False).wait_recv()
            down_pass(k, True).start()

    def down_wait():
        @pl.loop(0, NG // 2)
        def _(k):
            down_pass(k, False).wait_recv()

    def do_gain(i):
        for c in range(8 * i, 8 * i + 8):
            gain_col[c * 128 : (c + 1) * 128, :] = jnp.broadcast_to(gain[c : c + 1, :], (128, 128)).T

    def do_trig(s):
        index = lax.broadcasted_iota(jnp.int32, (HEAD // 2, ROWS), 0)
        fine, coarse = lax.rem(index, 8), lax.div(index, 8)
        fine_part = jnp.ones((HEAD // 2, ROWS), F32)
        coarse_part = fine_part
        for i in range(1, 8):
            fine_part = jnp.where(fine == i, float(rope_base ** (-2.0 * i / HEAD)), fine_part)
            coarse_part = jnp.where(coarse == i, float(rope_base ** (-16.0 * i / HEAD)), coarse_part)
        angle = pos[s : s + 1, aligned(xh * ROWS, ROWS, 128)].astype(F32) * (fine_part * coarse_part)
        trig[0, :, lanes(s)] = jnp.cos(angle)
        trig[1, :, lanes(s)] = jnp.sin(angle)

    def do_kv(i, j):
        if j == 0:
            kv_f[...] = kv_buf[i].astype(F32)
        for c in range(4 * j, 4 * j + 4):
            kv_t[i, c] = kv_f[:, c, :].T

    def do_w(x, i):
        part = pl.ds(i * 1024, 1024)
        w_raw[x, part, :] = (w_raw[x, part, :].astype(F32) * gain_col[part, :]).astype(BF16)

    def do_sums():
        every = pl.ds(1, NG - 1)
        for copy in own_grads:
            copy.wait()
        pltpu.make_async_copy(gd_buf.at[every], gd_buf.at[every], g_r.at[0]).wait()
        pltpu.make_async_copy(gu_buf.at[every], gu_buf.at[every], g_r.at[1]).wait()
        down_sum = gd_buf[0].astype(F32)
        up_sum = gu_buf[0].astype(F32)
        for k in range(1, NG):
            down_sum += gd_buf[k].astype(F32)
            up_sum += gu_buf[k].astype(F32)
        down = adamw(dpar[...], dfir[...], dsec[...], down_sum)
        up = adamw(upar[...], ufir[...], usec[...], up_sum)
        new_down[...] = down
        new_up[...] = up
        up_both[:, aligned(xh * HEAD, HEAD, 128)] = up

        @pl.when(z == g)
        def _():
            pad_a[...] = jnp.zeros_like(pad_a)
            pad_a[:RANK, :FEAT] = down
            pad_a[RANK:, :FEAT] = down
            scaled = pad_a[...].T[:FEAT, :] * gain_col[aligned(t * FEAT, FEAT, 32), :]
            hi = scaled.astype(BF16).astype(F32)
            lane = lax.broadcasted_iota(jnp.int32, (FEAT, 2 * RANK), 1)
            down_t[aligned((2 * g + xh) * FEAT, FEAT, 32), :] = jnp.where(lane < RANK, hi, scaled - hi).astype(BF16)

            @pl.loop(1, NZ)
            def _(k):
                down_along(k).start()

        send_u(True).start()

    across = (((0,), (0,)), ((), ()))

    everything = pl.ds(0, TOK)

    def q_block(zi, part=everything):
        rows = aligned(zi * 2 * FEAT, 2 * FEAT, 64)
        block = hidden_all[rows, part]
        for x in range(2):
            query[x * HEAD : (x + 1) * HEAD, part] += lax.dot_general(
                w_raw[x, rows, :], block, across, preferred_element_type=F32)
        wide = block.astype(F32)
        square[:, part] += jnp.sum((wide * wide).reshape(2 * FEAT // 8, 8, part.size), axis=0)

    def low_block(zi, part=everything):
        rows = aligned(zi * 2 * FEAT, 2 * FEAT, 64)
        low[:, part] += lax.dot_general(
            down_t[rows, :], hidden_all[rows, part], across, preferred_element_type=F32)

    def clear():
        query[...] = jnp.zeros_like(query)
        low[...] = jnp.zeros_like(low)
        square[...] = jnp.zeros_like(square)

    def finish_query(h):
        part = lanes_half(h)
        inverse = lax.rsqrt(jnp.sum(square[:, part], axis=0, keepdims=True) * (1.0 / WIDTH) + norm_eps)
        delta = lax.dot_general(
            up_both[...], low[:RANK, part] + low[RANK:, part], across,
            precision=lax.Precision.HIGHEST, preferred_element_type=F32)
        query[:, part] = (query[:, part] + delta * float(1.0 / np.sqrt(RANK * WIDTH))) * inverse

    half = HEAD // 2

    def attend(s):
        qgain_col = jnp.broadcast_to(qgain[...], (HEAD, HEAD)).T
        for x in range(2):
            q = query[x * HEAD : (x + 1) * HEAD, lanes(s)]
            q = q * lax.rsqrt(jnp.sum(q * q, axis=0, keepdims=True) * (1.0 / HEAD) + norm_eps) * qgain_col
            cosine, sine = trig[0, :, lanes(s)], trig[1, :, lanes(s)]
            first, second = q[:half], q[half:]
            rotated = jnp.concatenate(
                [first * cosine - second * sine, second * cosine + first * sine], axis=0)
            rotated = rotated.astype(BF16).astype(F32)
            scores = jnp.concatenate(
                [jnp.sum(rotated * kv_t[0, c], axis=0, keepdims=True) for c in range(CACHE)], axis=0)
            scores = scores * float(1.0 / np.sqrt(HEAD))
            expo = jnp.exp(scores - jnp.max(scores, axis=0, keepdims=True))
            weights = (expo / jnp.sum(expo, axis=0, keepdims=True)).astype(BF16).astype(F32)
            total = weights[0:1] * kv_t[1, 0]
            for c in range(1, CACHE):
                total += weights[c : c + 1] * kv_t[1, c]
            heads_all[aligned((2 * z + x) * HEAD, HEAD, 128), lanes(s)] = total.astype(BF16)

    def o_start():
        result[...] = hidden_all[aligned(z * 2 * FEAT, 2 * FEAT, 64), :].astype(F32)

    def o_block(zi, part=everything):
        rows = aligned(zi * 2 * HEAD, 2 * HEAD, 256)
        result[:, part] += jnp.dot(o_all[:, rows], heads_all[rows, part], preferred_element_type=F32)

    def out_copy(s, x):
        return remote(
            out_buf.at[s], decoded.at[s, :, aligned(x * ROWS, ROWS, 128)],
            out_s.at[s], out_r.at[s], {"tensor": partner})

    def finish(s):
        o_block(zm(8), lanes(s))
        out_buf[s] = result[aligned(xo * FEAT, FEAT, 32), lanes(s)].astype(BF16)
        out_copy(s, xh).start()
        decoded[s, :, aligned(xh * ROWS, ROWS, 128)] = result[aligned(xh * FEAT, FEAT, 32), lanes(s)].astype(BF16)

    order = [lambda: z] + [lambda f=f, k=k: f(k) for k in range(1, 8) for f in (zm, zp)]

    def blocks(kind, first, last):
        def run():
            for i in range(first, last):
                kind(order[i]())

        return run

    def wait_small():
        for copy in small:
            copy.wait()

    def q_arrived():
        send_q(False).wait_recv()
        share_q(True).start()

    def q_shared():
        share_q(False).wait_recv()
        share_q(True).wait_send()

    def o_arrived():
        send_o(False).wait_recv()
        share_o(True).start()

    def o_shared():
        own_o.wait()
        share_o(False).wait_recv()

    def start_other():
        for h in range(2):
            hx(2 * h, False).wait_recv()
            hx(2 * h + 1, False).wait_recv()
            ring_start(0, 2 + h)

    def last_hidden(h):
        q_block(zm(8), lanes_half(h))
        low_block(zm(8), lanes_half(h))
        finish_query(h)
        for s in (2 * h, 2 * h + 1):
            attend(s)
            ring_start(1, s)

    ring_run(0, {
        (1, 0): [send_grads(5, 9), wait_small, lambda: do_gain(0)],
        (1, 1): [send_grads(9, 13)],
        (1, 2): [send_grads(13, 16), lambda: do_gain(1), lambda: do_gain(2)],
        (1, 3): [lambda: do_gain(3), lambda: do_gain(4)],
        (2, 0): [lambda: do_trig(0)],
        (2, 1): [lambda: do_trig(1)],
        (2, 2): [lambda: do_trig(2)],
        (2, 3): [lambda: do_trig(3)],
        (3, 0): [do_sums],
        (3, 1): [own_kv.wait, lambda: do_kv(0, 0)],
        (3, 2): [lambda: do_kv(0, 1)],
        (3, 3): [lambda: do_kv(1, 0)],
        (4, 0): [down_first_part],
        (4, 1): [lambda: do_kv(1, 1)],
        (4, 2): [own_q.wait, lambda: do_w(xh, 0), lambda: do_w(xh, 1)],
        (4, 3): [lambda: do_w(xh, 2), lambda: do_w(xh, 3)],
        (5, 0): [down_second_part, q_arrived],
        (5, 1): [lambda: down_share(2, True).start(), lambda: down_share(3, True).start(), lambda: do_w(xh, 4), clear],
        (5, 2): [lambda: down_share(4, True).start(), lambda: down_share(5, True).start(),
                 q_shared, lambda: do_w(xo, 0)],
        (5, 3): [lambda: down_share(6, True).start(), lambda: down_share(7, True).start(),
                 lambda: do_w(xo, 1), lambda: do_w(xo, 2)],
        (6, 0): [lambda: down_pass(0, True).start(), lambda: do_w(xo, 3), lambda: do_w(xo, 4)],
        (6, 1): [blocks(q_block, 0, 2)],
        (6, 2): [blocks(q_block, 2, 4)],
        (6, 3): [down_third_part, blocks(q_block, 4, 5)],
        (7, 0): [blocks(q_block, 5, 7)],
        (7, 1): [blocks(q_block, 7, 9)],
        (7, 2): [down_wait, blocks(q_block, 9, 11), blocks(low_block, 0, 1)],
        (7, 3): [blocks(low_block, 1, 6)],
        (8, 0): [blocks(low_block, 6, 11)],
        (8, 1): [blocks(q_block, 11, 13), blocks(low_block, 11, 13), lambda: send_u(False).wait_recv(),
                 blocks(q_block, 13, 15), blocks(low_block, 13, 15)],
        (8, 2): [lambda: last_hidden(0)],
        (8, 3): [lambda: last_hidden(1)],
    })
    ring_run(1, {
        (1, 0): [o_arrived],
        (1, 1): [o_start],
        (1, 3): [o_shared],
        (2, 0): [blocks(o_block, 0, 1)],
        (2, 2): [blocks(o_block, 1, 3)],
        (3, 0): [blocks(o_block, 3, 4)],
        (3, 2): [blocks(o_block, 4, 5)],
        (4, 0): [blocks(o_block, 5, 6)],
        (4, 2): [blocks(o_block, 6, 7)],
        (5, 0): [blocks(o_block, 7, 8)],
        (5, 2): [blocks(o_block, 8, 9)],
        (6, 0): [blocks(o_block, 9, 10)],
        (6, 2): [blocks(o_block, 10, 11)],
        (7, 0): [blocks(o_block, 11, 12)],
        (7, 2): [blocks(o_block, 12, 13)],
        (7, 3): [blocks(o_block, 13, 15)],
        (8, 0): [lambda: finish(0)],
        (8, 1): [lambda: finish(1)],
        (8, 2): [lambda: finish(2)],
        (8, 3): [lambda: finish(3)],
    })

    for phase in range(2):
        ring_end(phase)
    for s in range(STEPS):
        hx(s, True).wait_send()
    for copy in (send_q, send_o, share_o, send_u, down_cross):
        copy(True).wait_send()

    @pl.when(z == g)
    def _():
        @pl.loop(1, NZ)
        def _(k):
            down_along(k).wait_send()

    @pl.loop(1, NG)
    def _(k):
        for copy in grad_copies(k):
            copy.wait_send()

    down_pass(0, True).wait_send()

    @pl.loop(1, NG // 2)
    def _(k):
        down_share(k, True).wait_send()
        down_pass(k, True).wait_send()

    for s in range(STEPS):
        out_copy(s, xh).wait_send()
        out_copy(s, xo).wait_recv()


def hand_over(*refs):
    count = len(refs) // 2
    for source, target in zip(refs[:count], refs[count:]):
        target[...] = source[...]


def body(
    hidden_in, norm_gain, q_weight, q_gain, o_weight, kv_cache, positions, grad_down, grad_up,
    down_param, down_first, down_second, up_param, up_first, up_second,
):
    vmem = pl.BlockSpec(memory_space=pltpu.VMEM)
    anywhere = pl.BlockSpec(memory_space=pl.ANY)
    dma = pltpu.SemaphoreType.DMA
    shapes = (
        jax.ShapeDtypeStruct((RANK, FEAT), F32),
        jax.ShapeDtypeStruct((RANK, HEAD), F32),
        jax.ShapeDtypeStruct((STEPS, FEAT, 2 * ROWS), BF16),
    )
    results = pl.pallas_call(
        kernel,
        out_shape=shapes,
        in_specs=[anywhere] * 15,
        out_specs=(vmem, vmem, vmem),
        scratch_shapes=[
            pltpu.VMEM((WIDTH, TOK), BF16),
            pltpu.VMEM((HQ, TOK), BF16),
            pltpu.VMEM((2, WIDTH, HEAD), BF16),
            pltpu.VMEM((2 * FEAT, HQ), BF16),
            pltpu.VMEM((WIDTH, 2 * RANK), BF16),
            pltpu.VMEM((NG, RANK, FEAT), BF16),
            pltpu.VMEM((NG, RANK, HEAD), BF16),
            pltpu.VMEM((RANK, 2 * HEAD), F32),
            pltpu.VMEM((2, ROWS, CACHE, HEAD), BF16),
            pltpu.VMEM((ROWS, CACHE, HEAD), F32),
            pltpu.VMEM((2, CACHE, HEAD, ROWS), F32),
            pltpu.VMEM((2, HEAD // 2, TOK), F32),
            pltpu.VMEM((2 * HEAD, TOK), F32),
            pltpu.VMEM((2 * RANK, TOK), F32),
            pltpu.VMEM((8, TOK), F32),
            pltpu.VMEM((2 * FEAT, TOK), F32),
            pltpu.VMEM((WIDTH, 128), F32),
            pltpu.VMEM((2 * RANK, 256), F32),
            pltpu.VMEM((STEPS, FEAT, ROWS), BF16),
            pltpu.VMEM((WIDTH // 128, 128), F32),
            pltpu.VMEM((1, HEAD), F32),
            pltpu.VMEM((STEPS, 2 * ROWS), jnp.int32),
            pltpu.VMEM((RANK, FEAT), F32), pltpu.VMEM((RANK, FEAT), F32), pltpu.VMEM((RANK, FEAT), F32),
            pltpu.VMEM((RANK, HEAD), F32), pltpu.VMEM((RANK, HEAD), F32), pltpu.VMEM((RANK, HEAD), F32),
            dma((18,)),
            dma((STEPS,)), dma((STEPS,)),
            dma((5,)), dma((5,)),
            dma((2, 8, 4)), dma((2, 8, 4)), dma((2, 8, 4)), dma((2, 8, 4)),
            dma((NZ,)), dma((1,)), dma((1,)), dma((1,)),
            dma((NG // 2,)), dma((NG // 2,)), dma((NG // 2,)), dma((NG // 2,)),
            dma((2, NG)), dma((2,)),
            dma((STEPS,)), dma((STEPS,)),
        ],
        compiler_params=pltpu.CompilerParams(
            collective_id=0, has_side_effects=True, vmem_limit_bytes=56 * 1024 * 1024),
        cost_estimate=pl.CostEstimate(flops=3_000_000_000, bytes_accessed=10_000_000, transcendentals=100_000),
    )(
        jnp.transpose(hidden_in, (0, 2, 1)), norm_gain.reshape(WIDTH // 128, 128), q_weight,
        q_gain.reshape(1, HEAD), jnp.transpose(o_weight), kv_cache, positions, grad_down, grad_up,
        down_param, down_first, down_second, up_param, up_first, up_second,
    )
    new_down, new_up, decoded = pl.pallas_call(
        hand_over,
        out_shape=shapes,
        in_specs=[vmem] * 3,
        out_specs=(vmem,) * 3,
    )(*results)
    return new_down, new_up, jnp.transpose(decoded, (0, 2, 1))


def solution(mesh):
    in_specs = (
        P(None, "group", "tensor"),
        P(),
        P(None, "tensor"),
        P(),
        P(None, "tensor"),
        P(None, "group", None, None),
        P(None, "group"),
        P("group", None, "tensor"),
        P("group", None, "tensor"),
        P(None, "tensor"),
        P(None, "tensor"),
        P(None, "tensor"),
        P(None, "tensor"),
        P(None, "tensor"),
        P(None, "tensor"),
    )
    out_specs = (P(None, "tensor"), P(None, "tensor"), P(None, "group", "tensor"))
    return jax.shard_map(body, mesh=mesh, in_specs=in_specs, out_specs=out_specs, check_vma=False)
```

```python
import jax
import jax.numpy as jnp
import numpy as np
from jax import lax
from jax.experimental import pallas as pl
from jax.experimental.pallas import tpu as pltpu
from jax.sharding import PartitionSpec as P

beta_first = 0.9
beta_second = 0.999
first_fix = 0.9999734386
second_fix = 0.095207851
learn_rate = 0.5
decay_rate = 0.01
adam_eps = 1e-08
norm_eps = 1e-06
rope_base = 1000000.0

MESH = pl.DeviceIdType.MESH
F32 = jnp.float32
BF16 = jnp.bfloat16
NZ = 16
NG = 16
FEAT = 160
WIDTH = 5120
HEAD = 128
ROWS = 128
STEPS = 4
CACHE = 8
RANK = 64
TOK = STEPS * ROWS
HQ = 4096
PIECES = 16


def adamw(param, first, second, grad):
    first_new = beta_first * first + (1.0 - beta_first) * grad
    second_new = beta_second * second + (1.0 - beta_second) * grad * grad
    first_hat = first_new / first_fix
    second_hat = second_new / second_fix
    return param - learn_rate * (first_hat / (jnp.sqrt(second_hat) + adam_eps) + decay_rate * param)


def aligned(start, size, multiple):
    return pl.ds(pl.multiple_of(start, multiple), size)


def kernel(
    hid, gain_h, qw, qgain_h, ow, kv, pos_h, gdown, gup, dpar_h, dfir_h, dsec_h, upar_h, ufir_h, usec_h,
    new_down, new_up, decoded,
    hidden_all, heads_all, w_raw, o_all, down_t, gd_buf, gu_buf, up_both, kv_buf, kv_f, kv_t, trig, query, low,
    square, result, gain_col, pad_a, out_buf,
    gain, qgain, pos, dpar, dfir, dsec, upar, ufir, usec,
    local_sem, hx_s, hx_r, w_s, w_r, cw_s, cw_r, cc_s, cc_r,
    da_s, da_r, dx_s, dx_r, db_s, db_r, dc_s, dc_r, g_s, g_r, out_s, out_r,
):
    g = lax.axis_index("group")
    t = lax.axis_index("tensor")
    z = lax.div(t, 2)
    xh = lax.rem(t, 2)
    xo = 1 - xh
    core = lax.rem(g, 2)
    sibling = g + 1 - 2 * core
    partner = 2 * z + xo
    right = lax.rem(z + 1, NZ) * 2 + xh
    left = lax.rem(z + NZ - 1, NZ) * 2 + xh
    kvh = lax.div(t, 8)
    beside = {"group": lax.rem(g + NG // 2, NG), "tensor": partner}

    def zm(k):
        return lax.rem(z + 2 * NZ - k, NZ)

    def zp(k):
        return lax.rem(z + k, NZ)

    def remote(src, dst, s_sem, r_sem, device):
        return pltpu.make_async_remote_copy(
            src_ref=src, dst_ref=dst, send_sem=s_sem, recv_sem=r_sem, device_id=device, device_id_type=MESH)

    def lanes(s):
        return pl.ds(s * ROWS, ROWS)

    def lanes_half(h):
        return pl.ds(h * 2 * ROWS, 2 * ROWS)

    barrier = pltpu.get_barrier_semaphore()
    pl.semaphore_signal(barrier, inc=1, device_id={"tensor": partner}, device_id_type=MESH)
    pl.semaphore_signal(barrier, inc=1, device_id=beside, device_id_type=MESH)

    @pl.loop(1, NG)
    def _(k):
        pl.semaphore_signal(barrier, inc=1, device_id={"tensor": 2 * zp(k) + xh}, device_id_type=MESH)
        pl.semaphore_signal(barrier, inc=1, device_id={"group": lax.rem(g + k, NG)}, device_id_type=MESH)

    def own_hidden(s):
        return pltpu.make_async_copy(
            hid.at[s, :, aligned(xh * ROWS, ROWS, 128)],
            hidden_all.at[aligned((2 * z + xh) * FEAT, FEAT, 32), lanes(s)], local_sem.at[s])

    small = [pltpu.make_async_copy(a, b, local_sem.at[4 + i]) for i, (a, b) in enumerate((
        (gain_h, gain), (qgain_h, qgain), (pos_h, pos), (dpar_h, dpar), (dfir_h, dfir), (dsec_h, dsec),
        (upar_h, upar), (ufir_h, ufir), (usec_h, usec)))]
    own_grads = (pltpu.make_async_copy(gdown.at[0], gd_buf.at[0], local_sem.at[13]),
                 pltpu.make_async_copy(gup.at[0], gu_buf.at[0], local_sem.at[14]))
    own_kv = pltpu.make_async_copy(
        kv.at[:, aligned(xh * ROWS, ROWS, 128), :, aligned(kvh * HEAD, HEAD, 128)], kv_buf, local_sem.at[15])
    own_q = pltpu.make_async_copy(qw, w_raw.at[xh], local_sem.at[16])
    own_o = pltpu.make_async_copy(ow, o_all.at[aligned(xh * FEAT, FEAT, 32)], local_sem.at[17])
    for s in range(STEPS):
        own_hidden(s).start()
    for copy in small:
        copy.start()
    for copy in own_grads:
        copy.start()
    own_kv.start()
    own_q.start()
    own_o.start()
    for s in range(STEPS):
        own_hidden(s).wait()

    pl.semaphore_wait(barrier, 2 + 2 * (NG - 1))

    def hx(s, sent):
        return remote(
            hid.at[s, :, aligned(xo * ROWS, ROWS, 128)],
            hidden_all.at[aligned((2 * z + (xh if sent else xo)) * FEAT, FEAT, 32), lanes(s)],
            hx_s.at[s], hx_r.at[s], {"tensor": partner})

    def chunk(phase, zi, j):
        if phase == 0:
            x = xh if j < 2 else xo
            return hidden_all.at[aligned((2 * zi + x) * FEAT, FEAT, 32), lanes_half(j % 2)]
        return heads_all.at[aligned(zi * 2 * HEAD, 2 * HEAD, 256), lanes(j)]

    def ring(phase, k, j, forward, sent):
        back = 1 if sent else 0
        at = phase, k - 1, j
        if forward:
            source, s_sem, r_sem, peer = zm(k - back), cw_s.at[at], cw_r.at[at], right
        else:
            source, s_sem, r_sem, peer = zp(k - back), cc_s.at[at], cc_r.at[at], left
        block = chunk(phase, source, j)
        return remote(block, block, s_sem, r_sem, {"tensor": peer})

    def has(k, j, forward):
        return k < 8 or (j % 2 == 0) == forward

    def ring_start(phase, *which):
        for j in which:
            ring(phase, 1, j, True, True).start()
            ring(phase, 1, j, False, True).start()

    def ring_step(phase, k, j):
        for forward in (True, False):
            if has(k, j, forward):
                ring(phase, k, j, forward, False).wait_recv()
                if k < 8 and has(k + 1, j, forward):
                    ring(phase, k + 1, j, forward, True).start()

    def ring_run(phase, work):
        steps = [(k, j) for k in range(1, 9) for j in range(4)]
        if phase == 0:
            steps = [(1, 0), (1, 1)]
            for k in range(1, 8):
                steps += [(k + 1, 0), (k + 1, 1), (k, 2), (k, 3)]
            steps += [(8, 2), (8, 3)]
        for slot, (k, j) in enumerate(steps):
            ring_step(phase, k, j)
            if phase == 0:
                if slot == 1:
                    start_other()
                for i in range(PIECES):
                    if i * 12 // PIECES == slot:
                        q_piece(i)
                    if i + 12 == slot:
                        o_piece(i)
            for unit in work.get((slot // 4 + 1, slot % 4), ()):
                unit()

    def ring_end(phase):
        for k in range(1, 9):
            for j in range(4):
                for forward in (True, False):
                    if has(k, j, forward):
                        ring(phase, k, j, forward, True).wait_send()

    def grad_copies(k):
        peer = {"group": lax.rem(g + k, NG)}
        return (remote(gdown.at[0], gd_buf.at[k], g_s.at[0, k], g_r.at[0], peer),
                remote(gup.at[0], gu_buf.at[k], g_s.at[1, k], g_r.at[1], peer))

    for s in range(STEPS):
        hx(s, True).start()
    ring_start(0, 0, 1)

    def send_grads(first, last):
        def run():
            @pl.loop(first, last)
            def _(k):
                for copy in grad_copies(k):
                    copy.start()

        return run

    send_grads(1, 5)()

    def q_half(x, c):
        return w_raw.at[x, aligned(c * (WIDTH // 2), WIDTH // 2, 32)]

    def o_half(x, c):
        return o_all.at[aligned(x * FEAT, FEAT, 32), aligned(c * (HQ // 2), HQ // 2, 128)]

    def send_q(sent):
        return remote(qw.at[aligned(core * (WIDTH // 2), WIDTH // 2, 32)], q_half(xh if sent else xo, core),
                      w_s.at[0], w_r.at[0], beside)

    def q_piece(i):
        rows = aligned(core * (WIDTH // 2) + i * FEAT, FEAT, 32)
        remote(qw.at[rows], w_raw.at[xh, rows], w_s.at[0], w_r.at[0], beside).start()

    def o_piece(i):
        part = aligned(core * (HQ // 2) + i * 128, 128, 128)
        remote(ow.at[:, part], o_all.at[aligned(xh * FEAT, FEAT, 32), part], w_s.at[2], w_r.at[2], beside).start()

    def share_q(sent):
        return remote(q_half(xo, core), q_half(xo, core if sent else 1 - core),
                      w_s.at[1], w_r.at[1], {"group": sibling})

    def send_o(sent):
        return remote(ow.at[:, aligned(core * (HQ // 2), HQ // 2, 128)], o_half(xh if sent else xo, core),
                      w_s.at[2], w_r.at[2], beside)

    def share_o(sent):
        return remote(o_half(xo, core), o_half(xo, core if sent else 1 - core),
                      w_s.at[3], w_r.at[3], {"group": sibling})

    def send_u(sent):
        block = up_both.at[:, aligned((xh if sent else xo) * HEAD, HEAD, 128)]
        return remote(block, block, w_s.at[4], w_r.at[4], {"tensor": partner})


    def down_rows(zi, x):
        return down_t.at[aligned((2 * zi + x) * FEAT, FEAT, 32)]

    def down_pair(zi):
        return down_t.at[aligned(zi * 2 * FEAT, 2 * FEAT, 64)]

    def down_along(k):
        return remote(down_rows(g, xh), down_rows(g, xh), da_s.at[k], da_r.at[0], {"tensor": 2 * zp(k) + xh})

    def down_cross(sent):
        block = down_rows(g, xh if sent else xo)
        return remote(block, block, dx_s.at[0], dx_r.at[0], {"tensor": partner})

    def down_share(k, sent):
        block = down_pair(g if sent else lax.rem(g + NG - 2 * k, NG))
        return remote(block, block, db_s.at[k], db_r.at[k], {"group": lax.rem(g + 2 * k, NG)})

    def down_pass(k, sent):
        block = down_pair(lax.rem((g if sent else sibling) + NG - 2 * k, NG))
        return remote(block, block, dc_s.at[k], dc_r.at[k], {"group": sibling})

    def down_first_part():
        @pl.when(z != g)
        def _():
            down_along(1).wait_recv()

        down_cross(True).start()

    def down_second_part():
        down_cross(False).wait_recv()

        down_share(1, True).start()

    def down_third_part():
        @pl.loop(1, NG // 2)
        def _(k):
            down_share(k, False).wait_recv()
            down_pass(k, True).start()

    def down_wait():
        @pl.loop(0, NG // 2)
        def _(k):
            down_pass(k, False).wait_recv()

    def do_gain(i):
        for c in range(8 * i, 8 * i + 8):
            gain_col[c * 128 : (c + 1) * 128, :] = jnp.broadcast_to(gain[c : c + 1, :], (128, 128)).T

    def do_trig(s):
        index = lax.broadcasted_iota(jnp.int32, (HEAD // 2, ROWS), 0)
        fine, coarse = lax.rem(index, 8), lax.div(index, 8)
        fine_part = jnp.ones((HEAD // 2, ROWS), F32)
        coarse_part = fine_part
        for i in range(1, 8):
            fine_part = jnp.where(fine == i, float(rope_base ** (-2.0 * i / HEAD)), fine_part)
            coarse_part = jnp.where(coarse == i, float(rope_base ** (-16.0 * i / HEAD)), coarse_part)
        angle = pos[s : s + 1, aligned(xh * ROWS, ROWS, 128)].astype(F32) * (fine_part * coarse_part)
        trig[0, :, lanes(s)] = jnp.cos(angle)
        trig[1, :, lanes(s)] = jnp.sin(angle)

    def do_kv(i, j):
        if j == 0:
            kv_f[...] = kv_buf[i].astype(F32)
        for c in range(4 * j, 4 * j + 4):
            kv_t[i, c] = kv_f[:, c, :].T

    def do_w(x, i):
        part = pl.ds(i * 1024, 1024)
        w_raw[x, part, :] = (w_raw[x, part, :].astype(F32) * gain_col[part, :]).astype(BF16)

    def do_sums():
        every = pl.ds(1, NG - 1)
        for copy in own_grads:
            copy.wait()
        pltpu.make_async_copy(gd_buf.at[every], gd_buf.at[every], g_r.at[0]).wait()
        pltpu.make_async_copy(gu_buf.at[every], gu_buf.at[every], g_r.at[1]).wait()
        down_sum = gd_buf[0].astype(F32)
        up_sum = gu_buf[0].astype(F32)
        for k in range(1, NG):
            down_sum += gd_buf[k].astype(F32)
            up_sum += gu_buf[k].astype(F32)
        down = adamw(dpar[...], dfir[...], dsec[...], down_sum)
        up = adamw(upar[...], ufir[...], usec[...], up_sum)
        new_down[...] = down
        new_up[...] = up
        up_both[:, aligned(xh * HEAD, HEAD, 128)] = up

        @pl.when(z == g)
        def _():
            pad_a[...] = jnp.zeros_like(pad_a)
            pad_a[:RANK, :FEAT] = down
            pad_a[RANK:, :FEAT] = down
            scaled = pad_a[...].T[:FEAT, :] * gain_col[aligned(t * FEAT, FEAT, 32), :]
            hi = scaled.astype(BF16).astype(F32)
            lane = lax.broadcasted_iota(jnp.int32, (FEAT, 2 * RANK), 1)
            down_t[aligned((2 * g + xh) * FEAT, FEAT, 32), :] = jnp.where(lane < RANK, hi, scaled - hi).astype(BF16)

            @pl.loop(1, NZ)
            def _(k):
                down_along(k).start()

        send_u(True).start()

    across = (((0,), (0,)), ((), ()))

    everything = pl.ds(0, TOK)

    def q_block(zi, part=everything):
        rows = aligned(zi * 2 * FEAT, 2 * FEAT, 64)
        block = hidden_all[rows, part]
        for x in range(2):
            query[x * HEAD : (x + 1) * HEAD, part] += lax.dot_general(
                w_raw[x, rows, :], block, across, preferred_element_type=F32)
        wide = block.astype(F32)
        square[:, part] += jnp.sum((wide * wide).reshape(2 * FEAT // 8, 8, part.size), axis=0)

    def low_block(zi, part=everything):
        rows = aligned(zi * 2 * FEAT, 2 * FEAT, 64)
        low[:, part] += lax.dot_general(
            down_t[rows, :], hidden_all[rows, part], across, preferred_element_type=F32)

    def clear():
        query[...] = jnp.zeros_like(query)
        low[...] = jnp.zeros_like(low)
        square[...] = jnp.zeros_like(square)

    def finish_query(h):
        part = lanes_half(h)
        inverse = lax.rsqrt(jnp.sum(square[:, part], axis=0, keepdims=True) * (1.0 / WIDTH) + norm_eps)
        delta = lax.dot_general(
            up_both[...], low[:RANK, part] + low[RANK:, part], across,
            precision=lax.Precision.HIGHEST, preferred_element_type=F32)
        query[:, part] = (query[:, part] + delta * float(1.0 / np.sqrt(RANK * WIDTH))) * inverse

    half = HEAD // 2

    def attend(s):
        qgain_col = jnp.broadcast_to(qgain[...], (HEAD, HEAD)).T
        for x in range(2):
            q = query[x * HEAD : (x + 1) * HEAD, lanes(s)]
            q = q * lax.rsqrt(jnp.sum(q * q, axis=0, keepdims=True) * (1.0 / HEAD) + norm_eps) * qgain_col
            cosine, sine = trig[0, :, lanes(s)], trig[1, :, lanes(s)]
            first, second = q[:half], q[half:]
            rotated = jnp.concatenate(
                [first * cosine - second * sine, second * cosine + first * sine], axis=0)
            rotated = rotated.astype(BF16).astype(F32)
            scores = jnp.concatenate(
                [jnp.sum(rotated * kv_t[0, c], axis=0, keepdims=True) for c in range(CACHE)], axis=0)
            scores = scores * float(1.0 / np.sqrt(HEAD))
            expo = jnp.exp(scores - jnp.max(scores, axis=0, keepdims=True))
            weights = (expo / jnp.sum(expo, axis=0, keepdims=True)).astype(BF16).astype(F32)
            total = weights[0:1] * kv_t[1, 0]
            for c in range(1, CACHE):
                total += weights[c : c + 1] * kv_t[1, c]
            heads_all[aligned((2 * z + x) * HEAD, HEAD, 128), lanes(s)] = total.astype(BF16)

    def o_start():
        result[...] = hidden_all[aligned(z * 2 * FEAT, 2 * FEAT, 64), :].astype(F32)

    def o_block(zi, part=everything):
        rows = aligned(zi * 2 * HEAD, 2 * HEAD, 256)
        result[:, part] += jnp.dot(o_all[:, rows], heads_all[rows, part], preferred_element_type=F32)

    def out_copy(s, x):
        return remote(
            out_buf.at[s], decoded.at[s, :, aligned(x * ROWS, ROWS, 128)],
            out_s.at[s], out_r.at[s], {"tensor": partner})

    def finish(s):
        o_block(zm(8), lanes(s))
        out_buf[s] = result[aligned(xo * FEAT, FEAT, 32), lanes(s)].astype(BF16)
        out_copy(s, xh).start()
        decoded[s, :, aligned(xh * ROWS, ROWS, 128)] = result[aligned(xh * FEAT, FEAT, 32), lanes(s)].astype(BF16)

    order = [lambda: z] + [lambda f=f, k=k: f(k) for k in range(1, 8) for f in (zm, zp)]

    def blocks(kind, first, last):
        def run():
            for i in range(first, last):
                kind(order[i]())

        return run

    def wait_small():
        for copy in small:
            copy.wait()

    def q_arrived():
        send_q(False).wait_recv()
        share_q(True).start()

    def q_shared():
        share_q(False).wait_recv()
        share_q(True).wait_send()

    def o_arrived():
        send_o(False).wait_recv()
        share_o(True).start()

    def o_shared():
        own_o.wait()
        share_o(False).wait_recv()

    def start_other():
        for h in range(2):
            hx(2 * h, False).wait_recv()
            hx(2 * h + 1, False).wait_recv()
            ring_start(0, 2 + h)

    def last_hidden(h):
        q_block(zm(8), lanes_half(h))
        low_block(zm(8), lanes_half(h))
        finish_query(h)
        for s in (2 * h, 2 * h + 1):
            attend(s)
            ring_start(1, s)

    ring_run(0, {
        (1, 0): [send_grads(5, 9), wait_small, lambda: do_gain(0)],
        (1, 1): [send_grads(9, 13)],
        (1, 2): [send_grads(13, 16), lambda: do_gain(1), lambda: do_gain(2)],
        (1, 3): [lambda: do_gain(3), lambda: do_gain(4)],
        (2, 0): [lambda: do_trig(0)],
        (2, 1): [lambda: do_trig(1)],
        (2, 2): [lambda: do_trig(2)],
        (2, 3): [lambda: do_trig(3)],
        (3, 0): [own_kv.wait, lambda: do_kv(0, 0)],
        (3, 1): [do_sums],
        (3, 2): [lambda: do_kv(0, 1)],
        (3, 3): [lambda: do_kv(1, 0)],
        (4, 0): [],
        (4, 1): [lambda: do_kv(1, 1)],
        (4, 2): [down_first_part, own_q.wait, lambda: do_w(xh, 0), lambda: do_w(xh, 1)],
        (4, 3): [lambda: do_w(xh, 2), lambda: do_w(xh, 3)],
        (5, 0): [q_arrived],
        (5, 1): [down_second_part, lambda: down_share(2, True).start(), lambda: do_w(xh, 4), clear],
        (5, 2): [lambda: down_share(3, True).start(), lambda: down_share(4, True).start(), lambda: down_share(5, True).start(),
                 q_shared, lambda: do_w(xo, 0)],
        (5, 3): [lambda: down_share(6, True).start(), lambda: down_share(7, True).start(),
                 lambda: do_w(xo, 1), lambda: do_w(xo, 2)],
        (6, 0): [lambda: down_pass(0, True).start(), lambda: do_w(xo, 3), lambda: do_w(xo, 4)],
        (6, 1): [blocks(q_block, 0, 2)],
        (6, 2): [blocks(q_block, 2, 4)],
        (6, 3): [blocks(q_block, 4, 5)],
        (7, 0): [down_third_part, blocks(q_block, 5, 7)],
        (7, 1): [blocks(q_block, 7, 9)],
        (7, 2): [blocks(q_block, 9, 11)],
        (7, 3): [down_wait, blocks(low_block, 0, 6)],
        (8, 0): [blocks(low_block, 6, 11)],
        (8, 1): [blocks(q_block, 11, 13), blocks(low_block, 11, 13), lambda: send_u(False).wait_recv(),
                 blocks(q_block, 13, 15), blocks(low_block, 13, 15)],
        (8, 2): [lambda: last_hidden(0)],
        (8, 3): [lambda: last_hidden(1)],
    })
    ring_run(1, {
        (1, 0): [o_arrived],
        (1, 1): [o_start],
        (1, 3): [o_shared],
        (2, 0): [blocks(o_block, 0, 1)],
        (2, 2): [blocks(o_block, 1, 3)],
        (3, 0): [blocks(o_block, 3, 4)],
        (3, 2): [blocks(o_block, 4, 5)],
        (4, 0): [blocks(o_block, 5, 6)],
        (4, 2): [blocks(o_block, 6, 7)],
        (5, 0): [blocks(o_block, 7, 8)],
        (5, 2): [blocks(o_block, 8, 9)],
        (6, 0): [blocks(o_block, 9, 10)],
        (6, 2): [blocks(o_block, 10, 11)],
        (7, 0): [blocks(o_block, 11, 12)],
        (7, 2): [blocks(o_block, 12, 13)],
        (7, 3): [blocks(o_block, 13, 15)],
        (8, 0): [lambda: finish(0)],
        (8, 1): [lambda: finish(1)],
        (8, 2): [lambda: finish(2)],
        (8, 3): [lambda: finish(3)],
    })

    for phase in range(2):
        ring_end(phase)
    for s in range(STEPS):
        hx(s, True).wait_send()
    for copy in (send_q, send_o, share_o, send_u, down_cross):
        copy(True).wait_send()

    @pl.when(z == g)
    def _():
        @pl.loop(1, NZ)
        def _(k):
            down_along(k).wait_send()

    @pl.loop(1, NG)
    def _(k):
        for copy in grad_copies(k):
            copy.wait_send()

    down_pass(0, True).wait_send()

    @pl.loop(1, NG // 2)
    def _(k):
        down_share(k, True).wait_send()
        down_pass(k, True).wait_send()

    for s in range(STEPS):
        out_copy(s, xh).wait_send()
        out_copy(s, xo).wait_recv()


def hand_over(*refs):
    count = len(refs) // 2
    for source, target in zip(refs[:count], refs[count:]):
        target[...] = source[...]


def body(
    hidden_in, norm_gain, q_weight, q_gain, o_weight, kv_cache, positions, grad_down, grad_up,
    down_param, down_first, down_second, up_param, up_first, up_second,
):
    vmem = pl.BlockSpec(memory_space=pltpu.VMEM)
    anywhere = pl.BlockSpec(memory_space=pl.ANY)
    dma = pltpu.SemaphoreType.DMA
    shapes = (
        jax.ShapeDtypeStruct((RANK, FEAT), F32),
        jax.ShapeDtypeStruct((RANK, HEAD), F32),
        jax.ShapeDtypeStruct((STEPS, FEAT, 2 * ROWS), BF16),
    )
    results = pl.pallas_call(
        kernel,
        out_shape=shapes,
        in_specs=[anywhere] * 15,
        out_specs=(vmem, vmem, vmem),
        scratch_shapes=[
            pltpu.VMEM((WIDTH, TOK), BF16),
            pltpu.VMEM((HQ, TOK), BF16),
            pltpu.VMEM((2, WIDTH, HEAD), BF16),
            pltpu.VMEM((2 * FEAT, HQ), BF16),
            pltpu.VMEM((WIDTH, 2 * RANK), BF16),
            pltpu.VMEM((NG, RANK, FEAT), BF16),
            pltpu.VMEM((NG, RANK, HEAD), BF16),
            pltpu.VMEM((RANK, 2 * HEAD), F32),
            pltpu.VMEM((2, ROWS, CACHE, HEAD), BF16),
            pltpu.VMEM((ROWS, CACHE, HEAD), F32),
            pltpu.VMEM((2, CACHE, HEAD, ROWS), F32),
            pltpu.VMEM((2, HEAD // 2, TOK), F32),
            pltpu.VMEM((2 * HEAD, TOK), F32),
            pltpu.VMEM((2 * RANK, TOK), F32),
            pltpu.VMEM((8, TOK), F32),
            pltpu.VMEM((2 * FEAT, TOK), F32),
            pltpu.VMEM((WIDTH, 128), F32),
            pltpu.VMEM((2 * RANK, 256), F32),
            pltpu.VMEM((STEPS, FEAT, ROWS), BF16),
            pltpu.VMEM((WIDTH // 128, 128), F32),
            pltpu.VMEM((1, HEAD), F32),
            pltpu.VMEM((STEPS, 2 * ROWS), jnp.int32),
            pltpu.VMEM((RANK, FEAT), F32), pltpu.VMEM((RANK, FEAT), F32), pltpu.VMEM((RANK, FEAT), F32),
            pltpu.VMEM((RANK, HEAD), F32), pltpu.VMEM((RANK, HEAD), F32), pltpu.VMEM((RANK, HEAD), F32),
            dma((18,)),
            dma((STEPS,)), dma((STEPS,)),
            dma((5,)), dma((5,)),
            dma((2, 8, 4)), dma((2, 8, 4)), dma((2, 8, 4)), dma((2, 8, 4)),
            dma((NZ,)), dma((1,)), dma((1,)), dma((1,)),
            dma((NG // 2,)), dma((NG // 2,)), dma((NG // 2,)), dma((NG // 2,)),
            dma((2, NG)), dma((2,)),
            dma((STEPS,)), dma((STEPS,)),
        ],
        compiler_params=pltpu.CompilerParams(
            collective_id=0, has_side_effects=True, vmem_limit_bytes=56 * 1024 * 1024),
        cost_estimate=pl.CostEstimate(flops=3_000_000_000, bytes_accessed=10_000_000, transcendentals=100_000),
    )(
        jnp.transpose(hidden_in, (0, 2, 1)), norm_gain.reshape(WIDTH // 128, 128), q_weight,
        q_gain.reshape(1, HEAD), jnp.transpose(o_weight), kv_cache, positions, grad_down, grad_up,
        down_param, down_first, down_second, up_param, up_first, up_second,
    )
    new_down, new_up, decoded = pl.pallas_call(
        hand_over,
        out_shape=shapes,
        in_specs=[vmem] * 3,
        out_specs=(vmem,) * 3,
    )(*results)
    return new_down, new_up, jnp.transpose(decoded, (0, 2, 1))


def solution(mesh):
    in_specs = (
        P(None, "group", "tensor"),
        P(),
        P(None, "tensor"),
        P(),
        P(None, "tensor"),
        P(None, "group", None, None),
        P(None, "group"),
        P("group", None, "tensor"),
        P("group", None, "tensor"),
        P(None, "tensor"),
        P(None, "tensor"),
        P(None, "tensor"),
        P(None, "tensor"),
        P(None, "tensor"),
        P(None, "tensor"),
    )
    out_specs = (P(None, "tensor"), P(None, "tensor"), P(None, "group", "tensor"))
    return jax.shard_map(body, mesh=mesh, in_specs=in_specs, out_specs=out_specs, check_vma=False)
```
